128 devices in a mesh: gx: 16 (over z, x), gy: 8 (over y, core).
Axes of the slice: x: 4, y: 4, z: 4, core: 2. Of those that a mesh axis runs over, the one named last changes fastest.
Arguments:
- clm_block: int32 [1048576], P(('gx', 'gy')), may hold values from 0 to 127, as said below
- clm_cell: int32 [1048576], P(('gx', 'gy')), may hold values from 0 to 8191, as said below
- precip: float32 [1048576], P(('gx', 'gy')), may hold values from 0.05 to 2
- evap_demand: float32 [1048576], P(('gx', 'gy')), may hold values from 0.05 to 1
- root_share: float32 [10, 1048576], P(None, ('gx', 'gy')), may hold values from 0.05 to 1
- sat_before: float32 [10, 1048576], P(None, ('gx', 'gy')), may hold values from 0.2 to 1
- pressure: float32 [10, 512, 2048], P(None, 'gx', 'gy'), may hold values from -3 to 0.5
- conductivity: float32 [10, 512, 2048], P(None, 'gx', 'gy'), may hold values from 0.1 to 3
- porosity: float32 [10, 512, 2048], P(None, 'gx', 'gy'), may hold values from 0.25 to 0.5
- freeze_state: int32 [10, 512, 2048], P(None, 'gx', 'gy'), may hold values from 0 to 2
- land_mask: int32 [512, 2048], P('gx', 'gy'), may hold values 0 or 1
Outputs:
- new_pressure: float32 [10, 512, 2048], P(None, 'gx', 'gy')
- returned_sat: float32 [10, 1048576], P(None, ('gx', 'gy'))
The draws below stay inside these ranges and needn't reach their ends.
Inputs may be any that keep to these rules, and one draw needn't show every extreme that they name: Grid blocks are 32 x 256 columns, numbered with the second horizontal dimension fastest. Within one device's entries clm_block never falls; one device's entries name at most 96 columns of one block, and exactly that many for some blocks. `clm_cell`: together with clm_block, every grid column is named exactly once.
All inputs are finite; a program needn't handle non-finite values. No bound on the sum of `land_mask` on one device may be relied on, other than what follows from the above.
Results may differ from the reference program's by a relative error of at most 0.0002.
Values sent between devices are 32-bit elements; how exact they have to be, the bound alone decides.
A program may use at most 64 MiB of HBM per device.

```python
import math
import jax
import jax.numpy as jnp
from jax import lax

NZ = 10
CX = 32
CY = 256
NEWTON = 2
SWEEPS = 4
NX = 512
NY = 2048
COLS = 1048576
N_GX = 16
N_GY = 8


def column_places(key):
    devices = N_GX * N_GY
    block_cells = CX * CY
    average = block_cells // devices
    swing = average // 2
    base_key = jax.random.fold_in(key, 7)
    first_key, second_key = jax.random.split(base_key, 2)
    order = jax.random.permutation(first_key, devices)
    signs = jnp.where(order < devices // 2, 1, -1).astype(jnp.int32)
    senders = jnp.arange(devices, dtype=jnp.int32)[:, None]
    owners = jnp.arange(devices, dtype=jnp.int32)[None, :]
    counts = average + swing * signs[(owners - senders) % devices]
    offsets = jnp.cumsum(counts, axis=0) - counts
    places = jax.vmap(lambda single: jax.random.permutation(single, block_cells))(jax.random.split(second_key, devices))

    def one_sender(sender):
        row_counts = counts[sender]
        owner = jnp.repeat(jnp.arange(devices, dtype=jnp.int32), row_counts, total_repeat_length=block_cells)
        starts = jnp.cumsum(row_counts) - row_counts
        ranks = jnp.arange(block_cells, dtype=jnp.int32) - starts[owner]
        local_cell = places[owner, offsets[sender, owner] + ranks]
        return (owner.astype(jnp.int32), local_cell.astype(jnp.int32))
    owner_all, cell_all = lax.map(one_sender, jnp.arange(devices, dtype=jnp.int32))
    return (owner_all.reshape(-1).astype(jnp.int32), cell_all.reshape(-1).astype(jnp.int32))


def draw_clm_block(key, part):
    return column_places(key)[0]


def draw_clm_cell(key, part):
    return column_places(key)[1]


def with_ends(drawn, own_key, low, top_value):
    longest = drawn.shape.index(max(drawn.shape))
    spots = []
    for shift in (0, 1):
        where = [jax.random.randint(jax.random.fold_in(own_key, axis), (), 0, length) for axis, length in enumerate(drawn.shape)]
        where[longest] = (where[longest] + shift) % drawn.shape[longest]
        spots.append(tuple(where))
    return drawn.at[spots[0]].set(low).at[spots[1]].set(top_value)


def level_of(own_key, shape, cuts, smallest, largest):
    def one(axis_at, parts):
        steps = jax.random.uniform(jax.random.fold_in(jax.random.fold_in(own_key, 6), axis_at), (parts,), jnp.float32, smallest / len(cuts), largest / len(cuts))
        return jnp.repeat(jnp.exp(steps), shape[axis_at] // parts).reshape((-1,) + (1,) * (len(shape) - axis_at - 1))

    loudness = one(*cuts[0])
    for cut in cuts[1:]:
        loudness = loudness * one(*cut)
    return loudness


def setup_inputs(seed: int = 0) -> dict:
    arg_keys = jax.random.split(jax.random.key(seed), 12)
    return {
        "clm_block": draw_clm_block(jax.random.fold_in(arg_keys[11], 71), 0),
        "clm_cell": draw_clm_cell(jax.random.fold_in(arg_keys[11], 71), 0),
        "precip": jnp.clip(jnp.exp(math.log(2.0) - 3.6888794 * jax.random.uniform(arg_keys[2], (COLS,), jnp.float32) ** level_of(arg_keys[2], (COLS,), ((0, 128),), -0.2, 0.2)), 0.05, 2.0),
        "evap_demand": jnp.clip(jnp.exp(math.log(1.0) - 2.9957323 * jax.random.uniform(arg_keys[3], (COLS,), jnp.float32) ** level_of(arg_keys[3], (COLS,), ((0, 128),), -0.2, 0.2)), 0.05, 1.0),
        "root_share": jnp.clip(0.05 + 0.95 * jax.random.uniform(arg_keys[4], (NZ, COLS), jnp.float32) ** level_of(arg_keys[4], (NZ, COLS), ((1, 128),), -0.2, 0.2), 0.05, 1.0),
        "sat_before": jnp.clip(0.2 + 0.8 * jax.random.uniform(arg_keys[5], (NZ, COLS), jnp.float32) ** level_of(arg_keys[5], (NZ, COLS), ((1, 128),), -0.2, 0.2), 0.2, 1.0),
        "pressure": jnp.clip(-3.0 + 3.5 * jax.random.uniform(arg_keys[6], (NZ, NX, NY), jnp.float32) ** level_of(arg_keys[6], (NZ, NX, NY), ((1, 16), (2, 8)), -0.2, 0.2), -3.0, 0.5),
        "conductivity": jnp.clip(jnp.exp(math.log(3.0) - 3.4011974 * jax.random.uniform(arg_keys[7], (NZ, NX, NY), jnp.float32) ** level_of(arg_keys[7], (NZ, NX, NY), ((1, 16), (2, 8)), -0.2, 0.2)), 0.1, 3.0),
        "porosity": jnp.clip(0.25 + 0.25 * jax.random.uniform(arg_keys[8], (NZ, NX, NY), jnp.float32) ** level_of(arg_keys[8], (NZ, NX, NY), ((1, 16), (2, 8)), -0.2, 0.2), 0.25, 0.5),
        "freeze_state": with_ends(jax.random.randint(arg_keys[9], (NZ, NX, NY), 0, 3), jax.random.fold_in(arg_keys[9], 1), 0, 2).astype(jnp.int32),
        "land_mask": with_ends((jax.random.randint(arg_keys[10], (NX, NY), 0, 4) < 3).astype(jnp.int32), jax.random.fold_in(arg_keys[10], 1), 0, 1),
    }


OMEGA = 0.8
SIDE_CUTS = ((slice(0, -2), slice(1, -1)), (slice(2, None), slice(1, -1)), (slice(1, -1), slice(0, -2)), (slice(1, -1), slice(2, None)))

def saturation(field):
    dryness = jnp.maximum(-field, 0.0)
    return 1.0 / jnp.sqrt(1.0 + dryness * dryness)

def saturation_slope(field):
    dryness = jnp.maximum(-field, 0.0)
    inverse = 1.0 / jnp.sqrt(1.0 + dryness * dryness)
    return dryness * inverse * inverse * inverse

def frozen_factor(freeze_state):
    return jnp.where(freeze_state == 0, 1.0, jnp.where(freeze_state == 1, 0.2, 0.02)).astype(jnp.float32)

def mean_face(perm_one, perm_two, rel_one, rel_two):
    return perm_one * perm_two / (perm_one + perm_two) * (rel_one + rel_two)

def column_fluxes(precip, evap_demand, root_share, sat_before):
    weights = root_share * sat_before * sat_before
    total = 0.25 + lax.optimization_barrier(jnp.sum(weights, axis=0))
    uptake = evap_demand * weights / total
    infiltration = precip * (1.0 - sat_before[0] ** 3)
    topmost = jnp.concatenate([infiltration[None], jnp.zeros_like(uptake[1:])], axis=0)
    return topmost - uptake

def linearize(pressure_pad, perm_pad, stored_before, porosity, source):
    relative = saturation(pressure_pad) ** 3
    perm_mid = perm_pad[:, 1:-1, 1:-1]
    rel_mid = relative[:, 1:-1, 1:-1]
    middle = pressure_pad[:, 1:-1, 1:-1]
    sides = []
    lateral = jnp.zeros_like(middle)
    for first_cut, second_cut in SIDE_CUTS:
        side = mean_face(perm_mid, perm_pad[:, first_cut, second_cut], rel_mid, relative[:, first_cut, second_cut])
        sides.append(side)
        lateral = lateral + side * (middle - pressure_pad[:, first_cut, second_cut])
    vertical = mean_face(perm_mid[:-1], perm_mid[1:], rel_mid[:-1], rel_mid[1:])
    drainage = perm_mid[-1] * rel_mid[-1]
    zero_layer = jnp.zeros_like(middle[:1])
    down_flow = vertical * (middle[:-1] - middle[1:] + 1.0)
    outflow = jnp.concatenate([down_flow, drainage[None]], axis=0) - jnp.concatenate([zero_layer, down_flow], axis=0)
    residual = porosity * (saturation(middle) - stored_before) + lateral + outflow - source
    diagonal = porosity * saturation_slope(middle) + sides[0] + sides[1] + sides[2] + sides[3]
    diagonal = diagonal + jnp.concatenate([vertical, zero_layer], axis=0) + jnp.concatenate([zero_layer, vertical], axis=0)
    return (residual, diagonal, sides, vertical)

def neighbour_sum(field_pad, sides, vertical):
    total = jnp.zeros_like(sides[0])
    for side, cuts in zip(sides, SIDE_CUTS):
        total = total + side * field_pad[:, cuts[0], cuts[1]]
    middle = field_pad[:, 1:-1, 1:-1]
    zero_layer = jnp.zeros_like(middle[:1])
    below = jnp.concatenate([vertical * middle[1:], zero_layer], axis=0)
    above = jnp.concatenate([zero_layer, vertical * middle[:-1]], axis=0)
    return total + below + above

def pad_sides(field):
    return jnp.pad(field, ((0, 0), (1, 1), (1, 1)))

def reference(clm_block, clm_cell, precip, evap_demand, root_share, sat_before, pressure, conductivity, porosity, freeze_state, land_mask):
    grid_x = clm_block // N_GY * CX + clm_cell // CY
    grid_y = clm_block % N_GY * CY + clm_cell % CY
    clm_target = (grid_x * NY + grid_y).astype(jnp.int32)
    flux = column_fluxes(precip, evap_demand, root_share, sat_before)
    source = jnp.zeros((NZ, NX * NY), jnp.float32).at[:, clm_target].set(flux)
    source = source.reshape(NZ, NX, NY) * land_mask.astype(jnp.float32)[None]
    perm = conductivity * frozen_factor(freeze_state)
    perm_pad = pad_sides(perm)
    stored_before = saturation(pressure)
    pressure_now = pressure
    for newton_step in range(NEWTON):
        residual, diagonal, sides, vertical = linearize(pad_sides(pressure_now), perm_pad, stored_before, porosity, source)
        update = OMEGA * -residual / diagonal
        for sweep_turn in range(SWEEPS - 1):
            coupled = neighbour_sum(pad_sides(update), sides, vertical)
            update = update + OMEGA * (coupled - residual - diagonal * update) / diagonal
        pressure_now = pressure_now + update
    saturated = saturation(pressure_now).reshape(NZ, NX * NY)
    returned_sat = saturated[:, clm_target]
    return (pressure_now, returned_sat)
```

```python
import functools

import jax
import jax.numpy as jnp
from jax import lax
from jax.experimental import pallas as pl
from jax.experimental.pallas import tpu as pltpu
from jax.sharding import PartitionSpec as P

MESH = pl.DeviceIdType.MESH
F32, BF16, I32 = jnp.float32, jnp.bfloat16, jnp.int32

NZ = 10
CX = 32
CY = 256
GX = 16
GY = 8
DEVICES = GX * GY
COLUMNS = CX * CY
HALO = 8
ROWS = CX + 2 * HALO
LANES = CY + 128
OMEGA = 0.8
VMEM_LIMIT = 56 * 1024 * 1024

VMEM = pl.BlockSpec(memory_space=pltpu.VMEM)
SMEM = pl.BlockSpec(memory_space=pltpu.SMEM)


def iota(shape, dim):
    return lax.broadcasted_iota(I32, shape, dim)


def params(**extra):
    return pltpu.CompilerParams(vmem_limit_bytes=VMEM_LIMIT, **extra)


def owner_ends(block_ref, row):
    owners = iota((DEVICES, 128), 0)

    def count(j, total):
        piece = block_ref[:, pl.ds(pl.multiple_of(j * 128, 128), 128)]
        return total + jnp.where(piece <= owners, 1.0, 0.0)

    total = lax.fori_loop(0, COLUMNS // 128, count, jnp.zeros((DEVICES, 128), F32), unroll=4)
    row[...] = lax.dot_general(
        jnp.ones((8, 128), BF16), total.astype(BF16), (((1,), (1,)), ((), ())), preferred_element_type=F32
    ).astype(I32)


def column_fluxes(cell_ref, precip_ref, evap_ref, root_ref, sat_ref, payload):
    width = 512

    def chunk(j, carry):
        at = pl.ds(pl.multiple_of(j * width, width), width)
        sat = sat_ref[:, at]
        weights = root_ref[:, at] * sat * sat
        total = 0.25 + jnp.sum(weights, axis=0, keepdims=True)
        uptake = evap_ref[:, at] * weights / total
        top = sat[0:1]
        infiltration = precip_ref[:, at] * (1.0 - top * top * top)
        payload[0:NZ, at] = jnp.where(iota((NZ, width), 0) == 0, infiltration, 0.0) - uptake
        payload[NZ : NZ + 1, at] = cell_ref[:, at].astype(F32)
        return carry

    lax.fori_loop(0, COLUMNS // width, chunk, 0)
    payload[:, COLUMNS : COLUMNS + 256] = jnp.zeros((16, 256), F32)


def run_of(ends, owner):
    end = ends[0, owner]
    start = jnp.where(owner == 0, 0, ends[0, jnp.maximum(owner - 1, 0)])
    base = pl.multiple_of((start // 128) * 128, 128)
    return start, end, base, start - base


def prep_kernel(block_ref, cell_ref, precip_ref, evap_ref, root_ref, sat_ref, messages_ref, ends_ref, payload, ends, sem):
    owner_ends(block_ref, ends_ref)
    copy = pltpu.make_async_copy(ends_ref, ends, sem)
    copy.start()
    column_fluxes(cell_ref, precip_ref, evap_ref, root_ref, sat_ref, payload)
    copy.wait()
    lane = iota((16, 128), 1)
    row = iota((16, 128), 0)

    def one(owner, carry):
        start, end, base, shift = run_of(ends, owner)
        amount = jnp.where(shift == 0, 0, 128 - shift)
        first = pltpu.roll(payload[:, pl.ds(base, 128)], amount, 1)
        second = pltpu.roll(payload[:, pl.ds(pl.multiple_of(base + 128, 128), 128)], amount, 1)
        slab = jnp.where(lane < 128 - shift, first, second)
        messages_ref[owner] = jnp.where((row == NZ) & (lane >= end - start), -1.0, slab)
        return carry

    lax.fori_loop(0, DEVICES, one, 0, unroll=4)


def unroute_kernel(ends, answer_ref, out_ref, wide):
    lane = iota((16, 128), 1)

    def one(owner, carry):
        _, _, base, shift = run_of(ends, owner)
        slab = pltpu.roll(answer_ref[owner], shift, 1)
        here = pl.ds(base, 128)
        wide[:, here] = jnp.where(lane >= shift, slab, wide[:, here])
        wide[:, pl.ds(pl.multiple_of(base + 128, 128), 128)] = slab
        return carry

    lax.fori_loop(0, DEVICES, one, 0, unroll=4)
    out_ref[...] = wide[0:NZ, 0:COLUMNS]


def position():
    return lax.axis_index("gx"), lax.axis_index("gy")


def device_at(offset):
    gx, gy = position()
    flat = lax.rem(gx * GY + gy + offset, DEVICES)
    return flat // GY, lax.rem(flat, GY)


def neighbour(dx, dy):
    gx, gy = position()
    return lax.rem(gx + dx + GX, GX), lax.rem(gy + dy + GY, GY)


def greet_all():
    barrier = pltpu.get_barrier_semaphore()

    def greet(k, carry):
        pl.semaphore_signal(barrier, inc=1, device_id=device_at(k), device_id_type=MESH)
        return carry

    lax.fori_loop(1, DEVICES, greet, 0)
    pl.semaphore_wait(barrier, DEVICES - 1)


def send_all(source, target, rows, send_sem, recv_sem):
    gx, gy = position()
    me = gx * GY + gy

    def send(k, carry):
        to = device_at(k)
        pltpu.make_async_remote_copy(
            src_ref=source.at[to[0] * GY + to[1], pl.ds(0, rows)],
            dst_ref=target.at[me, pl.ds(0, rows)],
            send_sem=send_sem,
            recv_sem=recv_sem,
            device_id=to,
            device_id_type=MESH,
        ).start()
        return carry

    lax.fori_loop(1, DEVICES, send, 0)
    target[me] = source[me]


def wait_all(source, target, rows, send_sem, recv_sem):
    part = (pl.ds(0, DEVICES - 1), pl.ds(0, rows))
    pltpu.make_async_copy(source.at[part], target.at[part], recv_sem).wait()
    pltpu.make_async_copy(source.at[part], target.at[part], send_sem).wait()


SIDES = tuple((dx, dy) for dx in (-1, 0, 1) for dy in (-1, 0, 1) if (dx, dy) != (0, 0))


def halo_copies(block, strips, x_halo, y_halo, send_sem, recv_sem):
    copies = []
    for at, (dx, dy) in enumerate(SIDES):
        from_rows = {-1: pl.ds(0, HALO), 0: pl.ds(0, CX), 1: pl.ds(CX - HALO, HALO)}[dx]
        to_rows = {-1: pl.ds(ROWS - HALO, HALO), 0: pl.ds(HALO, CX), 1: pl.ds(0, HALO)}[dx]
        if dy == 0:
            source, target = block.at[:, :, from_rows, :], x_halo.at[0 if dx == 1 else 1]
        else:
            source = strips.at[0 if dy == -1 else 1, :, from_rows, :]
            target = y_halo.at[0 if dy == 1 else 1, :, to_rows, :]
        copies.append(
            pltpu.make_async_remote_copy(
                src_ref=source,
                dst_ref=target,
                send_sem=send_sem.at[at],
                recv_sem=recv_sem.at[at],
                device_id=neighbour(dx, dy),
                device_id_type=MESH,
            )
        )
    return copies


def first_exchange_kernel(messages, block, strips, incoming, x_halo, y_halo, sems, halo_send, halo_recv):
    greet_all()
    copies = halo_copies(block, strips, x_halo, y_halo, halo_send, halo_recv)
    send_all(messages, incoming, NZ + 1, sems.at[0], sems.at[1])
    for copy in copies:
        copy.start()
    wait_all(messages, incoming, NZ + 1, sems.at[0], sems.at[1])
    for copy in copies:
        copy.wait()


def halo_kernel(block, strips, x_halo, y_halo, halo_send, halo_recv):
    barrier = pltpu.get_barrier_semaphore()
    for dx, dy in SIDES:
        pl.semaphore_signal(barrier, inc=1, device_id=neighbour(dx, dy), device_id_type=MESH)
    pl.semaphore_wait(barrier, len(SIDES))
    copies = halo_copies(block, strips, x_halo, y_halo, halo_send, halo_recv)
    for copy in copies:
        copy.start()
    for copy in copies:
        copy.wait()


def reply_kernel(reply, answer, sems):
    greet_all()
    send_all(reply, answer, NZ, sems.at[0], sems.at[1])
    wait_all(reply, answer, NZ, sems.at[0], sems.at[1])


def pack_strips(block, at, strips):
    group = iota((CX, 128), 1) // HALO
    low = jnp.zeros((CX, 128), F32)
    high = jnp.zeros((CX, 128), F32)
    for k in range(NZ):
        low = jnp.where(group == k, pltpu.roll(block[at, k, :, 0:128], HALO * k, 1), low)
        high = jnp.where(group == k, pltpu.roll(block[at, k, :, CY - 128 : CY], HALO * (k + 1), 1), high)
    strips[0, at] = low
    strips[1, at] = high


def block_kernel(pressure_ref, conductivity_ref, porosity_ref, freeze_ref, block, strips):
    freeze = freeze_ref[...]
    factor = jnp.where(freeze == 0, 1.0, jnp.where(freeze == 1, 0.2, 0.02)).astype(F32)
    block[0] = conductivity_ref[...] * factor
    block[1] = porosity_ref[...]
    block[2] = pressure_ref[...]
    for at in range(3):
        pack_strips(block, at, strips)


def widen(block, at, x_halo, y_halo, wide):
    lane = iota((ROWS, 128), 1)
    for k in range(NZ):
        wide[k, HALO : HALO + CX, 0:CY] = block[at, k]
        wide[k, 0:HALO, 0:CY] = x_halo[0, at, k]
        wide[k, HALO + CX : ROWS, 0:CY] = x_halo[1, at, k]
        low = pltpu.roll(y_halo[0, at], 120 - HALO * k, 1)
        high = pltpu.roll(y_halo[1, at], (128 - HALO * k) % 128, 1)
        wide[k, :, CY:LANES] = jnp.where(lane < HALO, high, jnp.where(lane >= 128 - HALO, low, 0.0))


def compact(ref, group):
    lane = iota((16, 128), 1)
    first, second, third, fourth = (ref[group * 4 + i] for i in range(4))
    second = pltpu.roll(second, 96, 1)
    third = pltpu.roll(third, 64, 1)
    fourth = pltpu.roll(fourth, 32, 1)
    return (
        jnp.where(lane < 96, first, second),
        jnp.where(lane < 64, second, third),
        jnp.where(lane < 32, third, fourth),
    )


def places(tile):
    cell = tile[NZ : NZ + 1].astype(I32)
    return cell >> 8, cell & (CY - 1)


def hot(index, size):
    return jnp.where(iota((size, index.shape[1]), 0) == index, 1.0, 0.0).astype(BF16)


def scatter_kernel(incoming, mask_ref, block, strips, total):
    total[...] = jnp.zeros_like(total)

    def step(j, carry):
        tiles = compact(incoming, 2 * j) + compact(incoming, 2 * j + 1)
        high_parts, low_parts, right_parts = [], [], []
        for tile in tiles:
            at_x, at_y = places(tile)
            hot_x = hot(at_x, CX)
            high = tile.astype(BF16).astype(F32)
            low = tile - high
            for part, into in ((high, high_parts), (low, low_parts)):
                rows = []
                for k in range(NZ):
                    spread = jnp.broadcast_to(part[k : k + 1], (16, 128)).astype(BF16)
                    rows += [spread * hot_x[0:16], spread * hot_x[16:32]]
                into.append(jnp.concatenate(rows, axis=0))
            right_parts.append(hot(at_y, CY))
        left = jnp.concatenate(high_parts + low_parts, axis=1)
        right = jnp.concatenate(right_parts + right_parts, axis=1)
        total[...] += lax.dot_general(left, right, (((1,), (1,)), ((), ())), preferred_element_type=F32)
        return carry

    lax.fori_loop(0, DEVICES // 8, step, 0)
    mask = mask_ref[...].astype(F32)
    for k in range(NZ):
        block[0, k] = total[k * CX : (k + 1) * CX] * mask
    pack_strips(block, 0, strips)


def up(field, dim):
    return pltpu.roll(field, field.shape[dim] - 1, dim)


def down(field, dim):
    return pltpu.roll(field, 1, dim)


def dry_inverse(field):
    dryness = jnp.maximum(-field, 0.0)
    return dryness, lax.rsqrt(1.0 + dryness * dryness)


def joined(one, two):
    both = one + two
    return one * two / jnp.where(both > 0.0, both, 1.0)


def newton_kernel(
    block, x_halo, y_halo, source, source_x, source_y, incoming, pressure_out, reply,
    perm, porosity, p, src, stored, kr, hx, hy, hz, gx_, gy_, gz, scale, start, u, v,
):
    gx, gy = position()
    widen(block, 0, x_halo, y_halo, perm)
    widen(block, 1, x_halo, y_halo, porosity)
    widen(block, 2, x_halo, y_halo, p)
    widen(source, 0, source_x, source_y, src)
    zero = jnp.zeros((ROWS, LANES), F32)
    row, lane = iota((ROWS, LANES), 0), iota((ROWS, LANES), 1)
    outside = ((row < HALO) & (gx == 0)) | ((row >= HALO + CX) & (gx == GX - 1))
    outside = outside | ((lane >= CY + 64) & (gy == 0)) | ((lane >= CY) & (lane < CY + 64) & (gy == GY - 1))
    p[NZ] = zero
    kr[NZ] = zero
    gz[0] = zero
    gz[NZ] = zero
    for ref in (u, v):
        ref[0] = zero
        ref[NZ + 1] = zero

    def prepare(k, carry):
        perm[k] = jnp.where(outside, 0.0, perm[k])
        return carry

    lax.fori_loop(0, NZ, prepare, 0)

    def faces(k, carry):
        here = perm[k]
        hx[k] = joined(here, up(here, 0))
        hy[k] = joined(here, up(here, 1))
        stored[k] = dry_inverse(p[k])[1]
        return carry

    lax.fori_loop(0, NZ, faces, 0)

    def vertical_faces(k, carry):
        hz[k] = joined(perm[k], perm[k + 1])
        return carry

    lax.fori_loop(0, NZ - 1, vertical_faces, 0)

    def newton(step, carry):
        def relative(k, carry):
            inverse = dry_inverse(p[k])[1]
            kr[k] = inverse * inverse * inverse
            return carry

        lax.fori_loop(0, NZ, relative, 0)

        def linearize(k, flow_above, last):
            here, rel = p[k], kr[k]
            side_x = hx[k] * (rel + up(rel, 0))
            side_y = hy[k] * (rel + up(rel, 1))
            gx_[k] = side_x
            gy_[k] = side_y
            flow_x = side_x * (here - up(here, 0))
            flow_y = side_y * (here - up(here, 1))
            above = gz[k]
            if last:
                flow = perm[k] * rel
            else:
                below = hz[k] * (rel + kr[k + 1])
                gz[k + 1] = below
                flow = below * (here - p[k + 1] + 1.0)
            dryness, inverse = dry_inverse(here)
            residual = porosity[k] * (inverse - stored[k]) + (flow_x - down(flow_x, 0)) + (flow_y - down(flow_y, 1))
            residual = residual + flow - flow_above - src[k]
            diagonal = porosity[k] * (dryness * rel) + side_x + down(side_x, 0) + side_y + down(side_y, 1) + above
            if not last:
                diagonal = diagonal + below
            diagonal = jnp.where(diagonal > 0.0, diagonal, 1.0)
            factor = OMEGA / diagonal
            scale[k] = factor
            first = -residual * factor
            start[k] = first
            u[k + 1] = first
            return flow

        flow = lax.fori_loop(0, NZ - 1, lambda k, f: linearize(k, f, False), zero)
        linearize(NZ - 1, flow, True)
        for old, new in ((u, v), (v, u), (u, v)):

            def sweep(k, carry, old=old, new=new):
                here = old[k + 1]
                side_x, side_y = gx_[k], gy_[k]
                coupled = side_x * up(here, 0) + down(side_x * here, 0) + side_y * up(here, 1) + down(side_y * here, 1)
                coupled = coupled + gz[k] * old[k] + gz[k + 1] * old[k + 2]
                new[k + 1] = (1.0 - OMEGA) * here + start[k] + scale[k] * coupled
                return carry

            lax.fori_loop(0, NZ, sweep, 0)

        def advance(k, carry):
            p[k] = p[k] + v[k + 1]
            return carry

        lax.fori_loop(0, NZ, advance, 0)
        return carry

    lax.fori_loop(0, 2, newton, 0)
    parts = []
    for k in range(NZ):
        final = p[k, HALO : HALO + CX, 0:CY]
        pressure_out[k] = final
        parts.append(dry_inverse(final)[1])
    saturated = jnp.concatenate(parts, axis=0)
    high = saturated.astype(BF16)
    left = jnp.concatenate([high, (saturated - high.astype(F32)).astype(BF16)], axis=1)
    gather(left, incoming, reply)


def gather(left, incoming, reply):
    lane = iota((16, 128), 1)

    def step(group, carry):
        outs = []
        for tile in compact(incoming, group):
            at_x, at_y = places(tile)
            hot_y = hot(at_y, CY)
            both = jnp.concatenate([hot_y, hot_y], axis=0)
            lines = jnp.dot(left, both, preferred_element_type=F32)
            here = iota((CX, 128), 0) == at_x
            rows = [
                jnp.sum(jnp.where(here, lines[k * CX : (k + 1) * CX], 0.0), axis=0, keepdims=True) for k in range(NZ)
            ]
            outs.append(jnp.concatenate(rows + [jnp.zeros((16 - NZ, 128), F32)], axis=0))
        one, two, three = outs
        reply[group * 4] = one
        reply[group * 4 + 1] = pltpu.roll(jnp.where(lane >= 96, one, two), 32, 1)
        reply[group * 4 + 2] = pltpu.roll(jnp.where(lane >= 64, two, three), 64, 1)
        reply[group * 4 + 3] = pltpu.roll(three, 96, 1)
        return carry

    lax.fori_loop(0, DEVICES // 4, step, 0)


def shaped(*lengths):
    return jax.ShapeDtypeStruct(lengths, F32)


def call(kernel, outs, scratch, extra=None, ins=None, count=None):
    return pl.pallas_call(
        kernel,
        out_shape=outs,
        in_specs=ins or [VMEM] * count,
        out_specs=jax.tree.map(lambda _: VMEM, outs),
        scratch_shapes=scratch,
        compiler_params=params(**(extra or {})),
    )


def on_device(
    clm_block, clm_cell, precip, evap_demand, root_share, sat_before,
    pressure, conductivity, porosity, freeze_state, land_mask,
):
    flat = [a.reshape(1, COLUMNS) for a in (clm_block, clm_cell, precip, evap_demand)]
    slabs = shaped(DEVICES, 16, 128)
    dma = pltpu.SemaphoreType.DMA
    messages, ends = call(
        prep_kernel,
        (slabs, jax.ShapeDtypeStruct((8, 128), I32)),
        [pltpu.VMEM((16, COLUMNS + 256), F32), pltpu.SMEM((8, 128), I32), dma],
        count=6,
    )(*flat, root_share, sat_before)
    block, strips = call(block_kernel, (shaped(3, NZ, CX, CY), shaped(2, 3, CX, 128)), [], count=4)(
        pressure, conductivity, porosity, freeze_state
    )
    incoming, x_halo, y_halo = call(
        first_exchange_kernel,
        (slabs, shaped(2, 3, NZ, HALO, CY), shaped(2, 3, ROWS, 128)),
        [dma((2,)), dma((8,)), dma((8,))],
        dict(collective_id=0, has_side_effects=True),
        count=3,
    )(messages, block, strips)
    source, source_strips = call(
        scatter_kernel, (shaped(1, NZ, CX, CY), shaped(2, 1, CX, 128)), [pltpu.VMEM((NZ * CX, CY), F32)], count=2
    )(incoming, land_mask)
    source_x, source_y = call(
        halo_kernel,
        (shaped(2, 1, NZ, HALO, CY), shaped(2, 1, ROWS, 128)),
        [dma((8,)), dma((8,))],
        dict(collective_id=1, has_side_effects=True),
        count=2,
    )(source, source_strips)
    wide = lambda n: pltpu.VMEM((n, ROWS, LANES), F32)
    counts = (NZ, NZ, NZ + 1, NZ, NZ, NZ + 1, NZ, NZ, NZ, NZ, NZ, NZ + 1, NZ, NZ, NZ + 2, NZ + 2)
    new_pressure, reply = call(
        newton_kernel, (shaped(NZ, CX, CY), slabs), [wide(n) for n in counts], count=7
    )(block, x_halo, y_halo, source, source_x, source_y, incoming)
    answer = call(
        reply_kernel, slabs, [dma((2,))], dict(collective_id=2, has_side_effects=True), count=1
    )(reply)
    returned = call(
        unroute_kernel, shaped(NZ, COLUMNS), [pltpu.VMEM((16, COLUMNS + 256), F32)], ins=[SMEM, VMEM]
    )(ends, answer)
    return new_pressure, returned


def solution(mesh):
    both = P(("gx", "gy"))
    columns = P(None, ("gx", "gy"))
    grid = P(None, "gx", "gy")
    return jax.shard_map(
        on_device,
        mesh=mesh,
        in_specs=(both, both, both, both, columns, columns, grid, grid, grid, grid, P("gx", "gy")),
        out_specs=(grid, columns),
        check_vma=False,
    )
```

```python
import functools

import jax
import jax.numpy as jnp
from jax import lax
from jax.experimental import pallas as pl
from jax.experimental.pallas import tpu as pltpu
from jax.sharding import PartitionSpec as P

MESH = pl.DeviceIdType.MESH
F32, BF16, I32 = jnp.float32, jnp.bfloat16, jnp.int32

NZ = 10
CX = 32
CY = 256
GX = 16
GY = 8
DEVICES = GX * GY
GROUP = 16
GROUPS = DEVICES // GROUP
COLUMNS = CX * CY
HALO = 8
ROWS = CX + 2 * HALO
LANES = CY + 128
OMEGA = 0.8
VMEM_LIMIT = 56 * 1024 * 1024

VMEM = pl.BlockSpec(memory_space=pltpu.VMEM)
SMEM = pl.BlockSpec(memory_space=pltpu.SMEM)


def iota(shape, dim):
    return lax.broadcasted_iota(I32, shape, dim)


def params(**extra):
    return pltpu.CompilerParams(vmem_limit_bytes=VMEM_LIMIT, **extra)


def owner_ends(block_ref, row):
    owners = iota((DEVICES, 128), 0)

    def count(j, total):
        piece = block_ref[:, pl.ds(pl.multiple_of(j * 128, 128), 128)]
        return total + jnp.where(piece <= owners, 1.0, 0.0)

    total = lax.fori_loop(0, COLUMNS // 128, count, jnp.zeros((DEVICES, 128), F32), unroll=4)
    row[...] = lax.dot_general(
        jnp.ones((8, 128), BF16), total.astype(BF16), (((1,), (1,)), ((), ())), preferred_element_type=F32
    ).astype(I32)


def column_fluxes(cell_ref, precip_ref, evap_ref, root_ref, sat_ref, payload):
    width = 512

    def chunk(j, carry):
        at = pl.ds(pl.multiple_of(j * width, width), width)
        sat = sat_ref[:, at]
        weights = root_ref[:, at] * sat * sat
        total = 0.25 + jnp.sum(weights, axis=0, keepdims=True)
        uptake = evap_ref[:, at] * weights / total
        top = sat[0:1]
        infiltration = precip_ref[:, at] * (1.0 - top * top * top)
        payload[0:NZ, at] = jnp.where(iota((NZ, width), 0) == 0, infiltration, 0.0) - uptake
        payload[NZ : NZ + 1, at] = cell_ref[:, at].astype(F32)
        return carry

    lax.fori_loop(0, COLUMNS // width, chunk, 0)
    payload[:, COLUMNS : COLUMNS + 256] = jnp.zeros((16, 256), F32)


def run_of(ends, owner):
    end = ends[0, owner]
    start = jnp.where(owner == 0, 0, ends[0, jnp.maximum(owner - 1, 0)])
    base = pl.multiple_of((start // 128) * 128, 128)
    return start, end, base, start - base


def prep_kernel(block_ref, cell_ref, precip_ref, evap_ref, root_ref, sat_ref, messages_ref, ends_ref, payload, ends, sem):
    owner_ends(block_ref, ends_ref)
    copy = pltpu.make_async_copy(ends_ref, ends, sem)
    copy.start()
    column_fluxes(cell_ref, precip_ref, evap_ref, root_ref, sat_ref, payload)
    copy.wait()
    lane = iota((16, 128), 1)
    row = iota((16, 128), 0)

    def one(owner, carry):
        start, end, base, shift = run_of(ends, owner)
        amount = jnp.where(shift == 0, 0, 128 - shift)
        first = pltpu.roll(payload[:, pl.ds(base, 128)], amount, 1)
        second = pltpu.roll(payload[:, pl.ds(pl.multiple_of(base + 128, 128), 128)], amount, 1)
        slab = jnp.where(lane < 128 - shift, first, second)
        messages_ref[owner] = jnp.where((row == NZ) & (lane >= end - start), -1.0, slab)
        return carry

    lax.fori_loop(0, DEVICES, one, 0, unroll=4)


def unroute_kernel(ends, answer_ref, out_ref, wide):
    lane = iota((16, 128), 1)

    def one(owner, carry):
        _, _, base, shift = run_of(ends, owner)
        slab = pltpu.roll(answer_ref[owner], shift, 1)
        here = pl.ds(base, 128)
        wide[:, here] = jnp.where(lane >= shift, slab, wide[:, here])
        wide[:, pl.ds(pl.multiple_of(base + 128, 128), 128)] = slab
        return carry

    lax.fori_loop(0, DEVICES, one, 0, unroll=4)
    out_ref[...] = wide[0:NZ, 0:COLUMNS]


def position():
    return lax.axis_index("gx"), lax.axis_index("gy")


def device_at(offset):
    gx, gy = position()
    flat = lax.rem(gx * GY + gy + offset, DEVICES)
    return flat // GY, lax.rem(flat, GY)


def neighbour(dx, dy):
    gx, gy = position()
    return lax.rem(gx + dx + GX, GX), lax.rem(gy + dy + GY, GY)


def greet_all():
    barrier = pltpu.get_barrier_semaphore()

    def greet(k, carry):
        pl.semaphore_signal(barrier, inc=1, device_id=device_at(k), device_id_type=MESH)
        return carry

    lax.fori_loop(1, DEVICES, greet, 0)


def send_messages(messages, incoming, send_sem, recv_sems):
    def send(k, carry):
        to = device_at(k)
        pltpu.make_async_remote_copy(
            src_ref=messages.at[to[0] * GY + to[1], pl.ds(0, NZ + 1)],
            dst_ref=incoming.at[k, pl.ds(0, NZ + 1)],
            send_sem=send_sem,
            recv_sem=recv_sems.at[k // GROUP],
            device_id=to,
            device_id_type=MESH,
        ).start()
        return carry

    lax.fori_loop(1, DEVICES, send, 0)
    gx, gy = position()
    incoming[0] = messages[gx * GY + gy]


def wait_for(ref, first, count, rows, sem):
    part = ref.at[pl.ds(first, count), pl.ds(0, rows)]
    pltpu.make_async_copy(part, part, sem).wait()


def send_replies(reply, answer, first, last, send_sem, recv_sem):
    gx, gy = position()
    me = gx * GY + gy

    def send(k, carry):
        pltpu.make_async_remote_copy(
            src_ref=reply.at[k, pl.ds(0, NZ)],
            dst_ref=answer.at[me, pl.ds(0, NZ)],
            send_sem=send_sem,
            recv_sem=recv_sem,
            device_id=device_at(DEVICES - k),
            device_id_type=MESH,
        ).start()
        return carry

    lax.fori_loop(first, last, send, 0)


SIDES = tuple((dx, dy) for dx in (-1, 0, 1) for dy in (-1, 0, 1) if (dx, dy) != (0, 0))


def halo_copies(block, strips, x_halo, y_halo, send_sem, recv_sem):
    copies = []
    for at, (dx, dy) in enumerate(SIDES):
        from_rows = {-1: pl.ds(0, HALO), 0: pl.ds(0, CX), 1: pl.ds(CX - HALO, HALO)}[dx]
        to_rows = {-1: pl.ds(ROWS - HALO, HALO), 0: pl.ds(HALO, CX), 1: pl.ds(0, HALO)}[dx]
        if dy == 0:
            source, target = block.at[:, :, from_rows, :], x_halo.at[0 if dx == 1 else 1]
        else:
            source = strips.at[0 if dy == -1 else 1, :, from_rows, :]
            target = y_halo.at[0 if dy == 1 else 1, :, to_rows, :]
        copies.append(
            pltpu.make_async_remote_copy(
                src_ref=source,
                dst_ref=target,
                send_sem=send_sem.at[at],
                recv_sem=recv_sem.at[at],
                device_id=neighbour(dx, dy),
                device_id_type=MESH,
            )
        )
    return copies


def pack_strips(block, at, strips):
    group = iota((CX, 128), 1) // HALO
    low = jnp.zeros((CX, 128), F32)
    high = jnp.zeros((CX, 128), F32)
    for k in range(NZ):
        low = jnp.where(group == k, pltpu.roll(block[at, k, :, 0:128], HALO * k, 1), low)
        high = jnp.where(group == k, pltpu.roll(block[at, k, :, CY - 128 : CY], HALO * (k + 1), 1), high)
    strips[0, at] = low
    strips[1, at] = high


def make_block(pressure_ref, conductivity_ref, porosity_ref, freeze_ref, block, strips):
    for k in range(NZ):
        freeze = freeze_ref[k]
        factor = jnp.where(freeze == 0, 1.0, jnp.where(freeze == 1, 0.2, 0.02)).astype(F32)
        block[0, k] = conductivity_ref[k] * factor
        block[1, k] = porosity_ref[k]
        block[2, k] = pressure_ref[k]
    for at in range(3):
        pack_strips(block, at, strips)


def widen(block, at, x_halo, y_halo, wide):
    lane = iota((ROWS, 128), 1)
    for k in range(NZ):
        wide[k, HALO : HALO + CX, 0:CY] = block[at, k]
        wide[k, 0:HALO, 0:CY] = x_halo[0, at, k]
        wide[k, HALO + CX : ROWS, 0:CY] = x_halo[1, at, k]
        low = pltpu.roll(y_halo[0, at], 120 - HALO * k, 1)
        high = pltpu.roll(y_halo[1, at], (128 - HALO * k) % 128, 1)
        wide[k, :, CY:LANES] = jnp.where(lane < HALO, high, jnp.where(lane >= 128 - HALO, low, 0.0))


def compact(ref, group):
    lane = iota((16, 128), 1)
    first, second, third, fourth = (ref[group * 4 + i] for i in range(4))
    second = pltpu.roll(second, 96, 1)
    third = pltpu.roll(third, 64, 1)
    fourth = pltpu.roll(fourth, 32, 1)
    return (
        jnp.where(lane < 96, first, second),
        jnp.where(lane < 64, second, third),
        jnp.where(lane < 32, third, fourth),
    )


def places(tile):
    cell = tile[NZ : NZ + 1].astype(I32)
    return cell >> 8, cell & (CY - 1)


def hot(index, size):
    rows = iota((size, index.shape[1]), 0).astype(F32).astype(BF16)
    marks = jnp.broadcast_to(index.astype(F32), (16, index.shape[1])).astype(BF16)
    marks = jnp.concatenate([marks] * (size // 16), axis=0)
    return jnp.where(rows == marks, jnp.ones((), BF16), jnp.zeros((), BF16))


def scatter_group(incoming, group, total):
    tiles = ()
    for i in range(GROUP // 4):
        tiles = tiles + compact(incoming, group * (GROUP // 4) + i)
    high_parts, low_parts, right_parts = [], [], []
    for tile in tiles:
        at_x, at_y = places(tile)
        hot_x = hot(at_x, CX)
        high = tile.astype(BF16).astype(F32)
        low = tile - high
        for part, into in ((high, high_parts), (low, low_parts)):
            rows = []
            for k in range(NZ):
                spread = jnp.broadcast_to(part[k : k + 1], (16, 128)).astype(BF16)
                rows += [spread * hot_x[0:16], spread * hot_x[16:32]]
            into.append(jnp.concatenate(rows, axis=0))
        right_parts.append(hot(at_y, CY))
    left = jnp.concatenate(high_parts + low_parts, axis=1)
    right = jnp.concatenate(right_parts + right_parts, axis=1)
    total[...] += lax.dot_general(left, right, (((1,), (1,)), ((), ())), preferred_element_type=F32)


def keep_source(total, mask_ref, source, strips):
    mask = mask_ref[...].astype(F32)
    for k in range(NZ):
        source[0, k] = total[k * CX : (k + 1) * CX] * mask
    pack_strips(source, 0, strips)


def up(field, dim):
    return pltpu.roll(field, field.shape[dim] - 1, dim)


def down(field, dim):
    return pltpu.roll(field, 1, dim)


def dry_inverse(field):
    dryness = jnp.maximum(-field, 0.0)
    return dryness, lax.rsqrt(1.0 + dryness * dryness)


def joined(one, two):
    both = one + two
    return one * two / jnp.where(both > 0.0, both, 1.0)


def grid_edges(wide_shape):
    gx, gy = position()
    row, lane = iota(wide_shape, 0), iota(wide_shape, 1)
    outside = ((row < HALO) & (gx == 0)) | ((row >= HALO + CX) & (gx == GX - 1))
    return outside | ((lane >= CY + 64) & (gy == 0)) | ((lane >= CY) & (lane < CY + 64) & (gy == GY - 1))


def zero_ends(p, kr, gz, u, v):
    zero = jnp.zeros((ROWS, LANES), F32)
    for ref, at in ((p, NZ), (kr, NZ), (gz, 0), (gz, NZ), (u, 0), (u, NZ + 1), (v, 0), (v, NZ + 1)):
        ref[at] = zero


def make_faces(perm, p, stored, hx, hy, hz):
    outside = grid_edges((ROWS, LANES))

    def prepare(k, carry):
        perm[k] = jnp.where(outside, 0.0, perm[k])
        return carry

    lax.fori_loop(0, NZ, prepare, 0)

    def faces(k, carry):
        here = perm[k]
        hx[k] = joined(here, up(here, 0))
        hy[k] = joined(here, up(here, 1))
        stored[k] = dry_inverse(p[k])[1]
        return carry

    lax.fori_loop(0, NZ, faces, 0)

    def vertical_faces(k, carry):
        hz[k] = joined(perm[k], perm[k + 1])
        return carry

    lax.fori_loop(0, NZ - 1, vertical_faces, 0)


def linearize(perm, porosity, p, stored, kr, hx, hy, hz, gx_, gy_, gz, scale, start):
    def relative(k, carry):
        inverse = dry_inverse(p[k])[1]
        kr[k] = inverse * inverse * inverse
        return carry

    lax.fori_loop(0, NZ, relative, 0)

    def layer(k, flow_above, last):
        here, rel = p[k], kr[k]
        side_x = hx[k] * (rel + up(rel, 0))
        side_y = hy[k] * (rel + up(rel, 1))
        gx_[k] = side_x
        gy_[k] = side_y
        flow_x = side_x * (here - up(here, 0))
        flow_y = side_y * (here - up(here, 1))
        above = gz[k]
        if last:
            flow = perm[k] * rel
        else:
            below = hz[k] * (rel + kr[k + 1])
            gz[k + 1] = below
            flow = below * (here - p[k + 1] + 1.0)
        dryness, inverse = dry_inverse(here)
        residual = porosity[k] * (inverse - stored[k]) + (flow_x - down(flow_x, 0)) + (flow_y - down(flow_y, 1))
        start[k] = residual + flow - flow_above
        diagonal = porosity[k] * (dryness * rel) + side_x + down(side_x, 0) + side_y + down(side_y, 1) + above
        if not last:
            diagonal = diagonal + below
        scale[k] = OMEGA / jnp.where(diagonal > 0.0, diagonal, 1.0)
        return flow

    flow = lax.fori_loop(0, NZ - 1, lambda k, f: layer(k, f, False), jnp.zeros((ROWS, LANES), F32))
    layer(NZ - 1, flow, True)


def smooth(p, src, gx_, gy_, gz, scale, start, u, v):
    def first(k, carry):
        opening = (src[k] - start[k]) * scale[k]
        start[k] = opening
        u[k + 1] = opening
        return carry

    lax.fori_loop(0, NZ, first, 0)
    for old, new in ((u, v), (v, u), (u, v)):

        def sweep(k, carry, old=old, new=new):
            here = old[k + 1]
            side_x, side_y = gx_[k], gy_[k]
            coupled = side_x * up(here, 0) + down(side_x * here, 0) + side_y * up(here, 1) + down(side_y * here, 1)
            coupled = coupled + gz[k] * old[k] + gz[k + 1] * old[k + 2]
            new[k + 1] = (1.0 - OMEGA) * here + start[k] + scale[k] * coupled
            return carry

        lax.fori_loop(0, NZ, sweep, 0)

    def advance(k, carry):
        p[k] = p[k] + v[k + 1]
        return carry

    lax.fori_loop(0, NZ, advance, 0)


def finish(p, pressure_out, saturated):
    for k in range(NZ):
        final = p[k, HALO : HALO + CX, 0:CY]
        pressure_out[k] = final
        rows = pl.ds(k, CX, stride=8) if k < 8 else pl.ds(CX * 8 + k - 8, CX, stride=2)
        sat = dry_inverse(final)[1]
        saturated[0, rows, :] = sat[:, 0:128]
        saturated[1, rows, :] = sat[:, 128:256]


def gather_group(saturated, incoming, group, reply):
    lane = iota((16, 128), 1)
    row = iota((8, 128), 0)
    every = jnp.concatenate([saturated[0], saturated[1]], axis=1)
    high = every.astype(BF16)
    left = jnp.concatenate([high, (every - high.astype(F32)).astype(BF16)], axis=1)
    for pair in range(GROUP // 8):
        at = group * (GROUP // 4) + 2 * pair
        tiles = compact(incoming, at) + compact(incoming, at + 1)
        spots = [places(tile) for tile in tiles]
        outs = []
        for i in range(3):
            two = jnp.concatenate([hot(spots[2 * i][1], CY), hot(spots[2 * i + 1][1], CY)], axis=1)
            both = jnp.concatenate([two, two], axis=0)
            lines = jnp.dot(left, both, preferred_element_type=F32)
            for half in range(2):
                part = lines[:, half * 128 : half * 128 + 128]
                at_x = jnp.broadcast_to(spots[2 * i + half][0], (8, 128))
                first = part[0:8]
                for x in range(1, CX):
                    first = jnp.where(at_x == x, part[8 * x : 8 * x + 8], first)
                second = part[256:264]
                for g in range(1, 8):
                    second = jnp.where((at_x >> 2) == g, part[256 + 8 * g : 264 + 8 * g], second)
                second = jnp.where((row >> 1) == (at_x & 3), second, 0.0)
                second = second + pltpu.roll(second, 4, 0)
                second = second + pltpu.roll(second, 2, 0)
                outs.append(jnp.concatenate([first, second], axis=0))
        for j in range(2):
            one, two, three = outs[3 * j : 3 * j + 3]
            base = group * GROUP + pair * 8 + j * 4
            reply[base] = one
            reply[base + 1] = pltpu.roll(jnp.where(lane >= 96, one, two), 32, 1)
            reply[base + 2] = pltpu.roll(jnp.where(lane >= 64, two, three), 64, 1)
            reply[base + 3] = pltpu.roll(three, 96, 1)


def interval_kernel(
    messages, pressure_ref, conductivity_ref, porosity_ref, freeze_ref, mask_ref, pressure_out, answer,
    incoming, reply, saturated, total, block, strips, x_halo, y_halo, source, source_strips, source_x, source_y,
    perm, porosity, p, src, stored, kr, hx, hy, hz, gx_, gy_, gz, scale, start, u, v,
    sems, group_sems, halo_send, halo_recv, source_send, source_recv,
):
    greet_all()
    make_block(pressure_ref, conductivity_ref, porosity_ref, freeze_ref, block, strips)
    pl.semaphore_wait(pltpu.get_barrier_semaphore(), DEVICES - 1)
    halos = halo_copies(block, strips, x_halo, y_halo, halo_send, halo_recv)
    for copy in halos:
        copy.start()
    send_messages(messages, incoming, sems.at[0], group_sems)
    zero_ends(p, kr, gz, u, v)
    total[...] = jnp.zeros_like(total)
    for copy in halos:
        copy.wait_recv()
    widen(block, 0, x_halo, y_halo, perm)
    widen(block, 1, x_halo, y_halo, porosity)
    widen(block, 2, x_halo, y_halo, p)
    make_faces(perm, p, stored, hx, hy, hz)
    linearize(perm, porosity, p, stored, kr, hx, hy, hz, gx_, gy_, gz, scale, start)
    wait_for(incoming, 1, GROUP - 1, NZ + 1, group_sems.at[0])
    scatter_group(incoming, 0, total)

    def arrive(group, carry):
        wait_for(incoming, group * GROUP, GROUP, NZ + 1, group_sems.at[group])
        scatter_group(incoming, group, total)
        return carry

    lax.fori_loop(1, GROUPS, arrive, 0)
    keep_source(total, mask_ref, source, source_strips)
    copies = halo_copies(source, source_strips, source_x, source_y, source_send, source_recv)
    for copy in copies:
        copy.start()
    for copy in copies:
        copy.wait_recv()
    widen(source, 0, source_x, source_y, src)
    smooth(p, src, gx_, gy_, gz, scale, start, u, v)
    linearize(perm, porosity, p, stored, kr, hx, hy, hz, gx_, gy_, gz, scale, start)
    smooth(p, src, gx_, gy_, gz, scale, start, u, v)
    finish(p, pressure_out, saturated)
    gather_group(saturated, incoming, 0, reply)
    send_replies(reply, answer, 1, GROUP, sems.at[1], sems.at[2])
    gx, gy = position()
    answer[gx * GY + gy] = reply[0]

    def depart(group, carry):
        gather_group(saturated, incoming, group, reply)
        send_replies(reply, answer, group * GROUP, group * GROUP + GROUP, sems.at[1], sems.at[2])
        return carry

    lax.fori_loop(1, GROUPS, depart, 0)
    for copy in halos + copies:
        copy.wait_send()
    wait_for(messages, 1, DEVICES - 1, NZ + 1, sems.at[0])
    wait_for(reply, 1, DEVICES - 1, NZ, sems.at[1])
    wait_for(answer, 1, DEVICES - 1, NZ, sems.at[2])


def shaped(*lengths):
    return jax.ShapeDtypeStruct(lengths, F32)


def call(kernel, outs, scratch, extra=None, ins=None, count=None):
    return pl.pallas_call(
        kernel,
        out_shape=outs,
        in_specs=ins or [VMEM] * count,
        out_specs=jax.tree.map(lambda _: VMEM, outs),
        scratch_shapes=scratch,
        compiler_params=params(**(extra or {})),
    )


def on_device(
    clm_block, clm_cell, precip, evap_demand, root_share, sat_before,
    pressure, conductivity, porosity, freeze_state, land_mask,
):
    flat = [a.reshape(1, COLUMNS) for a in (clm_block, clm_cell, precip, evap_demand)]
    slabs = shaped(DEVICES, 16, 128)
    dma = pltpu.SemaphoreType.DMA
    messages, ends = call(
        prep_kernel,
        (slabs, jax.ShapeDtypeStruct((8, 128), I32)),
        [pltpu.VMEM((16, COLUMNS + 256), F32), pltpu.SMEM((8, 128), I32), dma],
        count=6,
    )(*flat, root_share, sat_before)
    wide = [
        pltpu.VMEM((n, ROWS, LANES), F32)
        for n in (NZ, NZ, NZ + 1, NZ, NZ, NZ + 1, NZ, NZ, NZ, NZ, NZ, NZ + 1, NZ, NZ, NZ + 2, NZ + 2)
    ]
    memory = lambda *lengths: pltpu.VMEM(lengths, F32)
    new_pressure, answer = call(
        interval_kernel,
        (shaped(NZ, CX, CY), slabs),
        [memory(DEVICES, 16, 128), memory(DEVICES, 16, 128), memory(2, NZ * CX, 128), memory(NZ * CX, CY)]
        + [memory(3, NZ, CX, CY), memory(2, 3, CX, 128), memory(2, 3, NZ, HALO, CY), memory(2, 3, ROWS, 128)]
        + [memory(1, NZ, CX, CY), memory(2, 1, CX, 128), memory(2, 1, NZ, HALO, CY), memory(2, 1, ROWS, 128)]
        + wide
        + [dma((3,)), dma((GROUPS,)), dma((8,)), dma((8,)), dma((8,)), dma((8,))],
        dict(collective_id=0, has_side_effects=True),
        count=6,
    )(messages, pressure, conductivity, porosity, freeze_state, land_mask)
    returned = call(
        unroute_kernel, shaped(NZ, COLUMNS), [pltpu.VMEM((16, COLUMNS + 256), F32)], ins=[SMEM, VMEM]
    )(ends, answer)
    return new_pressure, returned


def solution(mesh):
    both = P(("gx", "gy"))
    columns = P(None, ("gx", "gy"))
    grid = P(None, "gx", "gy")
    return jax.shard_map(
        on_device,
        mesh=mesh,
        in_specs=(both, both, both, both, columns, columns, grid, grid, grid, grid, P("gx", "gy")),
        out_specs=(grid, columns),
        check_vma=False,
    )
```

```python
import functools

import jax
import jax.numpy as jnp
from jax import lax
from jax.experimental import pallas as pl
from jax.experimental.pallas import tpu as pltpu
from jax.sharding import PartitionSpec as P

MESH = pl.DeviceIdType.MESH
F32, BF16, I32 = jnp.float32, jnp.bfloat16, jnp.int32

NZ = 10
CX = 32
CY = 256
GX = 16
GY = 8
DEVICES = GX * GY
GROUP = 16
GROUPS = DEVICES // GROUP
SENT = 9
COLUMNS = CX * CY
HALO = 8
ROWS = CX + 2 * HALO
LANES = CY + 128
OMEGA = 0.8
VMEM_LIMIT = 56 * 1024 * 1024

VMEM = pl.BlockSpec(memory_space=pltpu.VMEM)
SMEM = pl.BlockSpec(memory_space=pltpu.SMEM)


def iota(shape, dim):
    return lax.broadcasted_iota(I32, shape, dim)


def params(**extra):
    return pltpu.CompilerParams(vmem_limit_bytes=VMEM_LIMIT, **extra)


def owner_ends(block_ref, row):
    owners = iota((DEVICES, 128), 0)

    def count(j, total):
        piece = block_ref[:, pl.ds(pl.multiple_of(j * 128, 128), 128)]
        return total + jnp.where(piece <= owners, 1, 0)

    total = lax.fori_loop(0, COLUMNS // 128, count, jnp.zeros((DEVICES, 128), I32), unroll=4)
    row[...] = jnp.broadcast_to(jnp.sum(total.T, axis=0, keepdims=True), (8, 128))


def column_fluxes(cell_ref, precip_ref, evap_ref, root_ref, sat_ref, payload):
    width = 512

    def chunk(j, carry):
        at = pl.ds(pl.multiple_of(j * width, width), width)
        sat = sat_ref[:, at]
        weights = root_ref[:, at] * sat * sat
        total = 0.25 + jnp.sum(weights, axis=0, keepdims=True)
        uptake = evap_ref[:, at] * weights / total
        top = sat[0:1]
        infiltration = precip_ref[:, at] * (1.0 - top * top * top)
        payload[0:NZ, at] = jnp.where(iota((NZ, width), 0) == 0, infiltration, 0.0) - uptake
        payload[NZ : NZ + 1, at] = cell_ref[:, at].astype(F32)
        return carry

    lax.fori_loop(0, COLUMNS // width, chunk, 0)
    payload[:, COLUMNS : COLUMNS + 256] = jnp.zeros((16, 256), F32)


def fold_last_rows(payload, folded):
    row, lane = iota((8, 128), 0), iota((8, 128), 1)
    third = jnp.where(row >= 6, row - 6, jnp.where(row >= 3, row - 3, row))
    moved = 96 - 32 * third

    def tile(t, carry):
        before, before_last = carry
        at = pl.ds(pl.multiple_of(t * 128, 128), 128)
        rows = [jnp.broadcast_to(payload[k : k + 1, at], (8, 128)) for k in (8, 9, 10)]
        mixed = jnp.where(row < 3, rows[0], jnp.where(row < 6, rows[1], rows[2]))
        here = jnp.where(
            third == 0, pltpu.roll(mixed, 96, 1), jnp.where(third == 1, pltpu.roll(mixed, 64, 1), pltpu.roll(mixed, 32, 1))
        )
        last = pltpu.roll(rows[2], 32, 1)
        folded[0:8, at] = jnp.where(lane < moved, before, here)
        folded[8:16, at] = jnp.where(lane < 32, before_last, last)
        return here, last

    zero = jnp.zeros((8, 128), F32)
    lax.fori_loop(0, COLUMNS // 128 + 2, tile, (zero, zero), unroll=22)


def run_of(ends, owner):
    end = ends[0, owner]
    start = jnp.where(owner == 0, 0, ends[0, jnp.maximum(owner - 1, 0)])
    base = pl.multiple_of((start // 128) * 128, 128)
    return start, end, base, start - base


def make_messages(ends, payload, folded, messages):
    lane, row = iota((8, 128), 1), iota((8, 128), 0)
    place = jnp.where(lane >= 96, lane - 96 + 32 * (row - 6), 0)
    cells = (lane >= 96) & (row >= 6)

    def one(owner, carry):
        start, end, base, shift = run_of(ends, owner)
        amount = jnp.where(shift == 0, 0, 128 - shift)
        here, there = pl.ds(base, 128), pl.ds(pl.multiple_of(base + 128, 128), 128)
        cut = shift + 96
        first = pltpu.roll(jnp.where(lane < cut, payload[0:8, here], folded[0:8, here]), amount, 1)
        second = pltpu.roll(jnp.where(lane + 128 < cut, payload[0:8, there], folded[0:8, there]), amount, 1)
        slab = jnp.where(lane < 128 - shift, first, second)
        messages[owner, 0:8] = jnp.where(cells & (place >= end - start), -1.0, slab)
        first = pltpu.roll(folded[8:16, here], amount, 1)
        second = pltpu.roll(folded[8:16, there], amount, 1)
        slab = jnp.where(lane < 128 - shift, first, second)
        messages[owner, 8:16] = jnp.where(lane - 32 >= end - start, -1.0, slab)
        return carry

    lax.fori_loop(0, DEVICES, one, 0, unroll=16)


def prep_kernel(*refs):
    given, (messages, ends_out), held = refs[:6], refs[6:8], refs[8:14]
    payload, folded, ends, load_sems, ends_sem = refs[14:]
    loads = [pltpu.make_async_copy(one, kept, load_sems.at[i]) for i, (one, kept) in enumerate(zip(given, held))]
    for load in loads:
        load.start()
    loads[0].wait()
    owner_ends(held[0], ends_out)
    copy_ends = pltpu.make_async_copy(ends_out, ends, ends_sem)
    copy_ends.start()
    for load in loads[1:]:
        load.wait()
    column_fluxes(*held[1:], payload)
    fold_last_rows(payload, folded)
    copy_ends.wait()
    make_messages(ends, payload, folded, messages)


def unroute_kernel(ends, answer_ref, pressure_ref, pressure_out, out_ref, wide, wide_last, last):
    pressure_out[...] = pressure_ref[...]
    lane = iota((DEVICES, 128), 1)
    for k in range(2):
        thirds = [
            pltpu.roll(answer_ref[pl.ds(2 * third + k, DEVICES, stride=8), :], 32 * (third + 1), 1) for third in range(3)
        ]
        last[pl.ds(k, DEVICES, stride=8), :] = jnp.where(
            lane < 32, thirds[0], jnp.where(lane < 64, thirds[1], thirds[2])
        )
    lane = iota((8, 128), 1)

    def one(owner, carry):
        tile, tile_last, before, before_last, old = carry
        _, _, base, shift = run_of(ends, owner)
        at = pl.ds(pl.multiple_of(owner * 8, 8), 8)
        slab = pltpu.roll(answer_ref[at, :], shift, 1)
        slab_last = pltpu.roll(last[at, :], shift, 1)
        here, there = pl.ds(base, 128), pl.ds(pl.multiple_of(base + 128, 128), 128)
        tile = jnp.where(lane >= shift, slab, jnp.where(base == old, tile, before))
        tile_last = jnp.where(lane >= shift, slab_last, jnp.where(base == old, tile_last, before_last))
        wide[:, here] = tile
        wide_last[:, here] = tile_last
        wide[:, there] = slab
        wide_last[:, there] = slab_last
        return tile, tile_last, slab, slab_last, base

    zero = jnp.zeros((8, 128), F32)
    lax.fori_loop(0, DEVICES, one, (zero, zero, zero, zero, jnp.int32(0)), unroll=16)
    out_ref[0:8, :] = wide[:, 0:COLUMNS]
    out_ref[8:NZ, :] = wide_last[0:2, 0:COLUMNS]


def position():
    return lax.axis_index("gx"), lax.axis_index("gy")


def device_at(offset):
    gx, gy = position()
    flat = lax.rem(gx * GY + gy + offset, DEVICES)
    return flat // GY, lax.rem(flat, GY)


def neighbour(dx, dy):
    gx, gy = position()
    return lax.rem(gx + dx + GX, GX), lax.rem(gy + dy + GY, GY)


def greet_all():
    barrier = pltpu.get_barrier_semaphore()

    def greet(k, carry):
        pl.semaphore_signal(barrier, inc=1, device_id=device_at(k), device_id_type=MESH)
        return carry

    lax.fori_loop(1, DEVICES, greet, 0)


def send_messages(messages, incoming, group, send_sem, recv_sems):
    def send(k, carry):
        to = device_at(k)
        pltpu.make_async_remote_copy(
            src_ref=messages.at[to[0] * GY + to[1], pl.ds(0, SENT)],
            dst_ref=incoming.at[k, pl.ds(0, SENT)],
            send_sem=send_sem,
            recv_sem=recv_sems.at[group],
            device_id=to,
            device_id_type=MESH,
        ).start()
        return carry

    lax.fori_loop(max(group * GROUP, 1), (group + 1) * GROUP, send, 0)


def wait_for(ref, first, count, rows, sem):
    part = ref.at[pl.ds(first, count), pl.ds(0, rows)]
    pltpu.make_async_copy(part, part, sem).wait()


def send_replies(reply, answer, first, last, send_sem, recv_sem):
    gx, gy = position()
    me = gx * GY + gy

    def send(k, carry):
        pltpu.make_async_remote_copy(
            src_ref=reply.at[k, pl.ds(0, 8)],
            dst_ref=answer.at[me, pl.ds(0, 8)],
            send_sem=send_sem,
            recv_sem=recv_sem,
            device_id=device_at(DEVICES - k),
            device_id_type=MESH,
        ).start()
        return carry

    lax.fori_loop(first, last, send, 0)


SIDES = tuple((dx, dy) for dx in (-1, 0, 1) for dy in (-1, 0, 1) if (dx, dy) != (0, 0))


def halo_copies(block, strips, x_halo, y_halo, send_sem, recv_sem):
    copies = []
    for at, (dx, dy) in enumerate(SIDES):
        from_rows = {-1: pl.ds(0, HALO), 0: pl.ds(0, CX), 1: pl.ds(CX - HALO, HALO)}[dx]
        to_rows = {-1: pl.ds(ROWS - HALO, HALO), 0: pl.ds(HALO, CX), 1: pl.ds(0, HALO)}[dx]
        if dy == 0:
            source, target = block.at[:, :, from_rows, :], x_halo.at[0 if dx == 1 else 1]
        else:
            source = strips.at[0 if dy == -1 else 1, :, from_rows, :]
            target = y_halo.at[0 if dy == 1 else 1, :, to_rows, :]
        copies.append(
            pltpu.make_async_remote_copy(
                src_ref=source,
                dst_ref=target,
                send_sem=send_sem.at[at],
                recv_sem=recv_sem.at[at],
                device_id=neighbour(dx, dy),
                device_id_type=MESH,
            )
        )
    return copies


def pack_strips(block, at, strips):
    group = iota((CX, 128), 1) // HALO
    low = jnp.zeros((CX, 128), F32)
    high = jnp.zeros((CX, 128), F32)
    for k in range(NZ):
        low = jnp.where(group == k, pltpu.roll(block[at, k, :, 0:128], HALO * k, 1), low)
        high = jnp.where(group == k, pltpu.roll(block[at, k, :, CY - 128 : CY], HALO * (k + 1), 1), high)
    strips[0, at] = low
    strips[1, at] = high


def make_block(pressure_ref, conductivity_ref, porosity_ref, freeze_ref, block, strips):
    for k in range(NZ):
        freeze = freeze_ref[k]
        factor = jnp.where(freeze == 0, 1.0, jnp.where(freeze == 1, 0.2, 0.02)).astype(F32)
        block[0, k] = conductivity_ref[k] * factor
        block[1, k] = porosity_ref[k]
        block[2, k] = pressure_ref[k]
    for at in range(3):
        pack_strips(block, at, strips)


def widen(block, at, x_halo, y_halo, wide):
    lane = iota((ROWS, 128), 1)
    for k in range(NZ):
        wide[k, HALO : HALO + CX, 0:CY] = block[at, k]
        wide[k, 0:HALO, 0:CY] = x_halo[0, at, k]
        wide[k, HALO + CX : ROWS, 0:CY] = x_halo[1, at, k]
        low = pltpu.roll(y_halo[0, at], 120 - HALO * k, 1)
        high = pltpu.roll(y_halo[1, at], (128 - HALO * k) % 128, 1)
        wide[k, :, CY:LANES] = jnp.where(lane < HALO, high, jnp.where(lane >= 128 - HALO, low, 0.0))


def compact(ref, group):
    lane = iota((8, 128), 1)
    first, second, third, fourth = (ref[group * 4 + i, 0:8] for i in range(4))
    second = pltpu.roll(second, 96, 1)
    third = pltpu.roll(third, 64, 1)
    fourth = pltpu.roll(fourth, 32, 1)
    mains = (
        jnp.where(lane < 96, first, second),
        jnp.where(lane < 64, second, third),
        jnp.where(lane < 32, third, fourth),
    )
    quarter = iota((3, 128), 1) // 32
    tiles = []
    for t in range(3):
        rest = None
        for q in range(4):
            at = 4 * t + q
            piece = ref[group * 4 + at // 3, pl.ds(at % 3, 3, stride=3), :]
            if q < 3:
                piece = pltpu.roll(piece, 32 * (q + 1), 1)
            rest = piece if q == 0 else jnp.where(quarter == q, piece, rest)
        tiles.append((mains[t], rest))
    return tuple(tiles)


def places(tile):
    cell = tile[1][2:3].astype(I32)
    return cell >> 8, cell & (CY - 1)


def hot(index, size):
    rows = iota((size, index.shape[1]), 0).astype(F32).astype(BF16)
    marks = jnp.broadcast_to(index.astype(F32), (16, index.shape[1])).astype(BF16)
    marks = jnp.concatenate([marks] * (size // 16), axis=0)
    return jnp.where(rows == marks, jnp.ones((), BF16), jnp.zeros((), BF16))


def scatter_group(incoming, group, total):
    tiles = ()
    for i in range(GROUP // 4):
        tiles = tiles + compact(incoming, group * (GROUP // 4) + i)
    high_parts, low_parts, right_parts = [], [], []
    for tile in tiles:
        at_x, at_y = places(tile)
        hot_x = hot(at_x, CX)
        highs = [part.astype(BF16).astype(F32) for part in tile]
        lows = [part - high for part, high in zip(tile, highs)]
        for parts, into in ((highs, high_parts), (lows, low_parts)):
            rows = []
            for k in range(NZ):
                line = parts[0][k : k + 1] if k < 8 else parts[1][k - 8 : k - 7]
                spread = jnp.broadcast_to(line, (16, 128)).astype(BF16)
                rows += [spread * hot_x[0:16], spread * hot_x[16:32]]
            into.append(jnp.concatenate(rows, axis=0))
        right_parts.append(hot(at_y, CY))
    left = jnp.concatenate(high_parts + low_parts, axis=1)
    right = jnp.concatenate(right_parts + right_parts, axis=1)
    total[...] += lax.dot_general(left, right, (((1,), (1,)), ((), ())), preferred_element_type=F32)


def keep_source(total, mask_ref, source, strips):
    mask = mask_ref[...].astype(F32)
    for k in range(NZ):
        source[0, k] = total[k * CX : (k + 1) * CX] * mask
    pack_strips(source, 0, strips)


def up(field, dim):
    return pltpu.roll(field, field.shape[dim] - 1, dim)


def down(field, dim):
    return pltpu.roll(field, 1, dim)


def dry_inverse(field):
    dryness = jnp.maximum(-field, 0.0)
    return dryness, lax.rsqrt(1.0 + dryness * dryness)


def joined(one, two):
    both = one + two
    return one * two / jnp.where(both > 0.0, both, 1.0)


def grid_edges(wide_shape):
    gx, gy = position()
    row, lane = iota(wide_shape, 0), iota(wide_shape, 1)
    outside = ((row < HALO) & (gx == 0)) | ((row >= HALO + CX) & (gx == GX - 1))
    return outside | ((lane >= CY + 64) & (gy == 0)) | ((lane >= CY) & (lane < CY + 64) & (gy == GY - 1))


def zero_ends(p, kr, gz, u, v):
    zero = jnp.zeros((ROWS, LANES), F32)
    for ref, at in ((p, NZ), (kr, NZ), (gz, 0), (gz, NZ), (u, 0), (u, NZ + 1), (v, 0), (v, NZ + 1)):
        ref[at] = zero


def make_faces(perm, p, stored, hx, hy, hz):
    outside = grid_edges((ROWS, LANES))

    def prepare(k, carry):
        perm[k] = jnp.where(outside, 0.0, perm[k])
        return carry

    lax.fori_loop(0, NZ, prepare, 0)

    def faces(k, carry):
        here = perm[k]
        hx[k] = joined(here, up(here, 0))
        hy[k] = joined(here, up(here, 1))
        stored[k] = dry_inverse(p[k])[1]
        return carry

    lax.fori_loop(0, NZ, faces, 0)

    def vertical_faces(k, carry):
        hz[k] = joined(perm[k], perm[k + 1])
        return carry

    lax.fori_loop(0, NZ - 1, vertical_faces, 0)


def linearize(perm, porosity, p, stored, kr, hx, hy, hz, gx_, gy_, gz, scale, start):
    def relative(k, carry):
        inverse = dry_inverse(p[k])[1]
        kr[k] = inverse * inverse * inverse
        return carry

    lax.fori_loop(0, NZ, relative, 0)

    def layer(k, flow_above, last):
        here, rel = p[k], kr[k]
        side_x = hx[k] * (rel + up(rel, 0))
        side_y = hy[k] * (rel + up(rel, 1))
        gx_[k] = side_x
        gy_[k] = side_y
        flow_x = side_x * (here - up(here, 0))
        flow_y = side_y * (here - up(here, 1))
        above = gz[k]
        if last:
            flow = perm[k] * rel
        else:
            below = hz[k] * (rel + kr[k + 1])
            gz[k + 1] = below
            flow = below * (here - p[k + 1] + 1.0)
        dryness, inverse = dry_inverse(here)
        residual = porosity[k] * (inverse - stored[k]) + (flow_x - down(flow_x, 0)) + (flow_y - down(flow_y, 1))
        start[k] = residual + flow - flow_above
        diagonal = porosity[k] * (dryness * rel) + side_x + down(side_x, 0) + side_y + down(side_y, 1) + above
        if not last:
            diagonal = diagonal + below
        scale[k] = OMEGA / jnp.where(diagonal > 0.0, diagonal, 1.0)
        return flow

    flow = lax.fori_loop(0, NZ - 1, lambda k, f: layer(k, f, False), jnp.zeros((ROWS, LANES), F32))
    layer(NZ - 1, flow, True)


def smooth(p, src, gx_, gy_, gz, scale, start, u, v):
    def first(k, carry):
        opening = (src[k] - start[k]) * scale[k]
        start[k] = opening
        u[k + 1] = opening
        return carry

    lax.fori_loop(0, NZ, first, 0)
    for old, new in ((u, v), (v, u), (u, v)):

        def sweep(k, carry, old=old, new=new):
            here = old[k + 1]
            side_x, side_y = gx_[k], gy_[k]
            coupled = side_x * up(here, 0) + down(side_x * here, 0) + side_y * up(here, 1) + down(side_y * here, 1)
            coupled = coupled + gz[k] * old[k] + gz[k + 1] * old[k + 2]
            new[k + 1] = (1.0 - OMEGA) * here + start[k] + scale[k] * coupled
            return carry

        lax.fori_loop(0, NZ, sweep, 0)

    def advance(k, carry):
        p[k] = p[k] + v[k + 1]
        return carry

    lax.fori_loop(0, NZ, advance, 0)


def finish(p, pressure_out, saturated):
    for k in range(NZ):
        final = p[k, HALO : HALO + CX, 0:CY]
        pressure_out[k] = final
        rows = pl.ds(k, CX, stride=8) if k < 8 else pl.ds(CX * 8 + k - 8, CX, stride=2)
        sat = dry_inverse(final)[1]
        saturated[0, rows, :] = sat[:, 0:128]
        saturated[1, rows, :] = sat[:, 128:256]


def gather_group(saturated, incoming, group, reply):
    lane = iota((8, 128), 1)
    row = iota((8, 128), 0)
    every = jnp.concatenate([saturated[0], saturated[1]], axis=1)
    high = every.astype(BF16)
    left = jnp.concatenate([high, (every - high.astype(F32)).astype(BF16)], axis=1)
    for pair in range(GROUP // 8):
        at = group * (GROUP // 4) + 2 * pair
        tiles = compact(incoming, at) + compact(incoming, at + 1)
        spots = [places(tile) for tile in tiles]
        outs = []
        for i in range(3):
            two = jnp.concatenate([hot(spots[2 * i][1], CY), hot(spots[2 * i + 1][1], CY)], axis=1)
            both = jnp.concatenate([two, two], axis=0)
            lines = jnp.dot(left, both, preferred_element_type=F32)
            for half in range(2):
                part = lines[:, half * 128 : half * 128 + 128]
                at_x = jnp.broadcast_to(spots[2 * i + half][0], (8, 128))
                first = part[0:8]
                for x in range(1, CX):
                    first = jnp.where(at_x == x, part[8 * x : 8 * x + 8], first)
                second = part[256:264]
                for g in range(1, 8):
                    second = jnp.where((at_x >> 2) == g, part[256 + 8 * g : 264 + 8 * g], second)
                second = jnp.where((row >> 1) == (at_x & 3), second, 0.0)
                second = second + pltpu.roll(second, 4, 0)
                second = second + pltpu.roll(second, 2, 0)
                outs.append((first, second))
        for j in range(2):
            three = outs[3 * j : 3 * j + 3]
            mains, rests = [m for m, _ in three], [r for _, r in three]
            mains = (
                mains[0],
                pltpu.roll(jnp.where(lane >= 96, mains[0], mains[1]), 32, 1),
                pltpu.roll(jnp.where(lane >= 64, mains[1], mains[2]), 64, 1),
                pltpu.roll(mains[2], 96, 1),
            )
            for i in range(4):
                slab = mains[i]
                for third in range(3):
                    at = 3 * i + third
                    piece = rests[at // 4]
                    if at % 4 < 3:
                        piece = pltpu.roll(piece, 96 - 32 * (at % 4), 1)
                    slab = jnp.where((lane >= 96) & (row >> 1 == third), piece, slab)
                reply[group * GROUP + pair * 8 + j * 4 + i] = slab


def interval_kernel(*refs):
    given, (pressure_out, answer), held, refs = refs[:6], refs[6:8], refs[8:14], refs[14:]
    (
        incoming, reply, saturated, total, block, strips, x_halo, y_halo,
        source, source_strips, source_x, source_y,
        perm, porosity, p, src, stored, kr, hx, hy, hz, gx_, gy_, gz, scale, start, u, v,
        load_sems, sems, group_sems, halo_send, halo_recv, source_send, source_recv,
    ) = refs
    messages, mask_ref = held[0], held[5]
    loads = [pltpu.make_async_copy(one, kept, load_sems.at[i]) for i, (one, kept) in enumerate(zip(given, held))]
    for load in loads[1:] + loads[:1]:
        load.start()
    greet_all()
    for load in loads[1:]:
        load.wait()
    make_block(*held[1:5], block, strips)
    loads[0].wait()
    pl.semaphore_wait(pltpu.get_barrier_semaphore(), DEVICES - 1)
    halos = halo_copies(block, strips, x_halo, y_halo, halo_send, halo_recv)
    for group in range(GROUPS):
        send_messages(messages, incoming, group, sems.at[0], group_sems)
    for copy in halos:
        copy.start()
    gx, gy = position()
    incoming[0] = messages[gx * GY + gy]
    zero_ends(p, kr, gz, u, v)
    total[...] = jnp.zeros_like(total)
    wait_for(incoming, 1, GROUP - 1, SENT, group_sems.at[0])
    scatter_group(incoming, 0, total)

    def arrive(group, carry):
        wait_for(incoming, group * GROUP, GROUP, SENT, group_sems.at[group])
        scatter_group(incoming, group, total)
        return carry

    lax.fori_loop(1, GROUPS, arrive, 0)
    keep_source(total, mask_ref, source, source_strips)
    copies = halo_copies(source, source_strips, source_x, source_y, source_send, source_recv)
    for copy in copies:
        copy.start()
    for copy in halos:
        copy.wait_recv()
    widen(block, 0, x_halo, y_halo, perm)
    widen(block, 1, x_halo, y_halo, porosity)
    widen(block, 2, x_halo, y_halo, p)
    make_faces(perm, p, stored, hx, hy, hz)
    linearize(perm, porosity, p, stored, kr, hx, hy, hz, gx_, gy_, gz, scale, start)
    for copy in copies:
        copy.wait_recv()
    widen(source, 0, source_x, source_y, src)
    smooth(p, src, gx_, gy_, gz, scale, start, u, v)
    linearize(perm, porosity, p, stored, kr, hx, hy, hz, gx_, gy_, gz, scale, start)
    smooth(p, src, gx_, gy_, gz, scale, start, u, v)
    finish(p, pressure_out, saturated)
    gather_group(saturated, incoming, 0, reply)
    send_replies(reply, answer, 1, GROUP, sems.at[1], sems.at[2])
    gx, gy = position()
    answer[gx * GY + gy] = reply[0]

    def depart(group, carry):
        gather_group(saturated, incoming, group, reply)
        send_replies(reply, answer, group * GROUP, group * GROUP + GROUP, sems.at[1], sems.at[2])
        return carry

    lax.fori_loop(1, GROUPS, depart, 0)
    for copy in halos + copies:
        copy.wait_send()
    wait_for(messages, 1, DEVICES - 1, SENT, sems.at[0])
    wait_for(reply, 1, DEVICES - 1, 8, sems.at[1])
    wait_for(answer, 1, DEVICES - 1, 8, sems.at[2])


def shaped(*lengths):
    return jax.ShapeDtypeStruct(lengths, F32)


def call(kernel, outs, scratch, extra=None, ins=None, count=None):
    return pl.pallas_call(
        kernel,
        out_shape=outs,
        in_specs=ins or [VMEM] * count,
        out_specs=jax.tree.map(lambda _: VMEM, outs),
        scratch_shapes=scratch,
        compiler_params=params(**(extra or {})),
    )


def on_device(
    clm_block, clm_cell, precip, evap_demand, root_share, sat_before,
    pressure, conductivity, porosity, freeze_state, land_mask,
):
    flat = [a.reshape(1, COLUMNS) for a in (clm_block, clm_cell, precip, evap_demand)]
    dma = pltpu.SemaphoreType.DMA
    wide = [
        pltpu.VMEM((n, ROWS, LANES), F32)
        for n in (NZ, NZ, NZ + 1, NZ, NZ, NZ + 1, NZ, NZ, NZ, NZ, NZ, NZ + 1, NZ, NZ, NZ + 2, NZ + 2)
    ]
    memory = lambda *lengths: pltpu.VMEM(lengths, F32)
    anywhere = pl.BlockSpec(memory_space=pl.ANY)
    held = lambda given: [pltpu.VMEM(a.shape, a.dtype) for a in given]
    given = (*flat, root_share, sat_before)
    messages, ends = call(
        prep_kernel,
        (shaped(DEVICES, 16, 128), jax.ShapeDtypeStruct((8, 128), I32)),
        held(given)
        + [memory(16, COLUMNS + 256), memory(16, COLUMNS + 256), pltpu.SMEM((8, 128), I32), dma((6,)), dma],
        ins=[anywhere] * 6,
    )(*given)
    given = (messages, pressure, conductivity, porosity, freeze_state, land_mask)
    pressure_now, answer = call(
        interval_kernel,
        (shaped(NZ, CX, CY), shaped(DEVICES, 8, 128)),
        held(given)
        + [memory(DEVICES, 16, 128), memory(DEVICES, 8, 128), memory(2, NZ * CX, 128), memory(NZ * CX, CY)]
        + [memory(3, NZ, CX, CY), memory(2, 3, CX, 128), memory(2, 3, NZ, HALO, CY), memory(2, 3, ROWS, 128)]
        + [memory(1, NZ, CX, CY), memory(2, 1, CX, 128), memory(2, 1, NZ, HALO, CY), memory(2, 1, ROWS, 128)]
        + wide
        + [dma((6,)), dma((3,)), dma((GROUPS,)), dma((8,)), dma((8,)), dma((8,)), dma((8,))],
        dict(collective_id=0, has_side_effects=True),
        ins=[anywhere] * 6,
    )(*given)
    new_pressure, returned = call(
        unroute_kernel,
        (shaped(NZ, CX, CY), shaped(NZ, COLUMNS)),
        [memory(8, COLUMNS + 256), memory(8, COLUMNS + 256), memory(DEVICES * 8, 128)],
        ins=[SMEM, VMEM, VMEM],
    )(ends, answer.reshape(DEVICES * 8, 128), pressure_now)
    return new_pressure, returned


def solution(mesh):
    both = P(("gx", "gy"))
    columns = P(None, ("gx", "gy"))
    grid = P(None, "gx", "gy")
    return jax.shard_map(
        on_device,
        mesh=mesh,
        in_specs=(both, both, both, both, columns, columns, grid, grid, grid, grid, P("gx", "gy")),
        out_specs=(grid, columns),
        check_vma=False,
    )
```

```python
import functools

import jax
import jax.numpy as jnp
from jax import lax
from jax.experimental import pallas as pl
from jax.experimental.pallas import tpu as pltpu
from jax.sharding import PartitionSpec as P

MESH = pl.DeviceIdType.MESH
F32, BF16, I32 = jnp.float32, jnp.bfloat16, jnp.int32

NZ = 10
CX = 32
CY = 256
GX = 16
GY = 8
DEVICES = GX * GY
GROUP = 16
GROUPS = DEVICES // GROUP
SENT = 9
COLUMNS = CX * CY
HALO = 8
ROWS = CX + 2 * HALO
LANES = CY + 128
OMEGA = 0.8
VMEM_LIMIT = 56 * 1024 * 1024

VMEM = pl.BlockSpec(memory_space=pltpu.VMEM)
SMEM = pl.BlockSpec(memory_space=pltpu.SMEM)


def iota(shape, dim):
    return lax.broadcasted_iota(I32, shape, dim)


def params(**extra):
    return pltpu.CompilerParams(vmem_limit_bytes=VMEM_LIMIT, **extra)


def owner_ends(block_ref, row):
    owners = iota((DEVICES, 128), 0)

    def count(j, total):
        piece = block_ref[:, pl.ds(pl.multiple_of(j * 128, 128), 128)]
        return total + jnp.where(piece <= owners, 1, 0)

    total = lax.fori_loop(0, COLUMNS // 128, count, jnp.zeros((DEVICES, 128), I32), unroll=4)
    row[...] = jnp.broadcast_to(jnp.sum(total.T, axis=0, keepdims=True), (8, 128))


def column_fluxes(cell_ref, precip_ref, evap_ref, root_ref, sat_ref, payload):
    width = 512

    def chunk(j, carry):
        at = pl.ds(pl.multiple_of(j * width, width), width)
        sat = sat_ref[:, at]
        weights = root_ref[:, at] * sat * sat
        total = 0.25 + jnp.sum(weights, axis=0, keepdims=True)
        uptake = evap_ref[:, at] * weights / total
        top = sat[0:1]
        infiltration = precip_ref[:, at] * (1.0 - top * top * top)
        payload[0:NZ, at] = jnp.where(iota((NZ, width), 0) == 0, infiltration, 0.0) - uptake
        payload[NZ : NZ + 1, at] = cell_ref[:, at].astype(F32)
        return carry

    lax.fori_loop(0, COLUMNS // width, chunk, 0)
    payload[:, COLUMNS : COLUMNS + 256] = jnp.zeros((16, 256), F32)


def fold_last_rows(payload, folded):
    row, lane = iota((8, 128), 0), iota((8, 128), 1)
    third = jnp.where(row >= 6, row - 6, jnp.where(row >= 3, row - 3, row))
    moved = 96 - 32 * third

    def tile(t, carry):
        before, before_last = carry
        at = pl.ds(pl.multiple_of(t * 128, 128), 128)
        rows = [jnp.broadcast_to(payload[k : k + 1, at], (8, 128)) for k in (8, 9, 10)]
        mixed = jnp.where(row < 3, rows[0], jnp.where(row < 6, rows[1], rows[2]))
        here = jnp.where(
            third == 0, pltpu.roll(mixed, 96, 1), jnp.where(third == 1, pltpu.roll(mixed, 64, 1), pltpu.roll(mixed, 32, 1))
        )
        last = pltpu.roll(rows[2], 32, 1)
        folded[0:8, at] = jnp.where(lane < moved, before, here)
        folded[8:16, at] = jnp.where(lane < 32, before_last, last)
        return here, last

    zero = jnp.zeros((8, 128), F32)
    lax.fori_loop(0, COLUMNS // 128 + 2, tile, (zero, zero), unroll=22)


def run_of(ends, owner):
    end = ends[0, owner]
    start = jnp.where(owner == 0, 0, ends[0, jnp.maximum(owner - 1, 0)])
    base = pl.multiple_of((start // 128) * 128, 128)
    return start, end, base, start - base


def make_messages(ends, payload, folded, messages):
    lane, row = iota((8, 128), 1), iota((8, 128), 0)
    place = jnp.where(lane >= 96, lane - 96 + 32 * (row - 6), 0)
    cells = (lane >= 96) & (row >= 6)

    def one(owner, carry):
        start, end, base, shift = run_of(ends, owner)
        amount = jnp.where(shift == 0, 0, 128 - shift)
        here, there = pl.ds(base, 128), pl.ds(pl.multiple_of(base + 128, 128), 128)
        cut = shift + 96
        first = pltpu.roll(jnp.where(lane < cut, payload[0:8, here], folded[0:8, here]), amount, 1)
        second = pltpu.roll(jnp.where(lane + 128 < cut, payload[0:8, there], folded[0:8, there]), amount, 1)
        slab = jnp.where(lane < 128 - shift, first, second)
        messages[owner, 0:8] = jnp.where(cells & (place >= end - start), -1.0, slab)
        first = pltpu.roll(folded[8:16, here], amount, 1)
        second = pltpu.roll(folded[8:16, there], amount, 1)
        slab = jnp.where(lane < 128 - shift, first, second)
        messages[owner, 8:16] = jnp.where(lane - 32 >= end - start, -1.0, slab)
        return carry

    lax.fori_loop(0, DEVICES, one, 0, unroll=16)


def prep_kernel(*refs):
    given, (messages, ends_out), held = refs[:6], refs[6:8], refs[8:14]
    payload, folded, ends, load_sems, ends_sem = refs[14:]
    loads = [pltpu.make_async_copy(one, kept, load_sems.at[i]) for i, (one, kept) in enumerate(zip(given, held))]
    for load in loads:
        load.start()
    loads[0].wait()
    owner_ends(held[0], ends_out)
    copy_ends = pltpu.make_async_copy(ends_out, ends, ends_sem)
    copy_ends.start()
    for load in loads[1:]:
        load.wait()
    column_fluxes(*held[1:], payload)
    fold_last_rows(payload, folded)
    copy_ends.wait()
    make_messages(ends, payload, folded, messages)


def unroute_kernel(ends, answer_ref, pressure_ref, pressure_out, out_ref, wide, wide_last, last):
    pressure_out[...] = pressure_ref[...]
    lane = iota((DEVICES, 128), 1)
    for k in range(2):
        thirds = [
            pltpu.roll(answer_ref[pl.ds(2 * third + k, DEVICES, stride=8), :], 32 * (third + 1), 1) for third in range(3)
        ]
        last[pl.ds(k, DEVICES, stride=8), :] = jnp.where(
            lane < 32, thirds[0], jnp.where(lane < 64, thirds[1], thirds[2])
        )
    lane = iota((8, 128), 1)

    def one(owner, carry):
        tile, tile_last, before, before_last, old = carry
        _, _, base, shift = run_of(ends, owner)
        at = pl.ds(pl.multiple_of(owner * 8, 8), 8)
        slab = pltpu.roll(answer_ref[at, :], shift, 1)
        slab_last = pltpu.roll(last[at, :], shift, 1)
        here, there = pl.ds(base, 128), pl.ds(pl.multiple_of(base + 128, 128), 128)
        tile = jnp.where(lane >= shift, slab, jnp.where(base == old, tile, before))
        tile_last = jnp.where(lane >= shift, slab_last, jnp.where(base == old, tile_last, before_last))
        wide[:, here] = tile
        wide_last[:, here] = tile_last
        wide[:, there] = slab
        wide_last[:, there] = slab_last
        return tile, tile_last, slab, slab_last, base

    zero = jnp.zeros((8, 128), F32)
    lax.fori_loop(0, DEVICES, one, (zero, zero, zero, zero, jnp.int32(0)), unroll=16)
    out_ref[0:8, :] = wide[:, 0:COLUMNS]
    out_ref[8:NZ, :] = wide_last[0:2, 0:COLUMNS]


def position():
    return lax.axis_index("gx"), lax.axis_index("gy")


def device_at(offset):
    gx, gy = position()
    flat = lax.rem(gx * GY + gy + offset, DEVICES)
    return flat // GY, lax.rem(flat, GY)


def neighbour(dx, dy):
    gx, gy = position()
    return lax.rem(gx + dx + GX, GX), lax.rem(gy + dy + GY, GY)


def greet_all():
    barrier = pltpu.get_barrier_semaphore()

    def greet(k, carry):
        pl.semaphore_signal(barrier, inc=1, device_id=device_at(k), device_id_type=MESH)
        return carry

    lax.fori_loop(1, DEVICES, greet, 0)


def send_messages(messages, incoming, group, send_sem, recv_sems):
    def send(k, carry):
        to = device_at(k)
        pltpu.make_async_remote_copy(
            src_ref=messages.at[to[0] * GY + to[1], pl.ds(0, SENT)],
            dst_ref=incoming.at[k, pl.ds(0, SENT)],
            send_sem=send_sem,
            recv_sem=recv_sems.at[group],
            device_id=to,
            device_id_type=MESH,
        ).start()
        return carry

    lax.fori_loop(max(group * GROUP, 1), (group + 1) * GROUP, send, 0)


def wait_for(ref, first, count, rows, sem):
    part = ref.at[pl.ds(first, count), pl.ds(0, rows)]
    pltpu.make_async_copy(part, part, sem).wait()


def send_replies(reply, answer, first, last, send_sem, recv_sem):
    gx, gy = position()
    me = gx * GY + gy

    def send(k, carry):
        pltpu.make_async_remote_copy(
            src_ref=reply.at[k, pl.ds(0, 8)],
            dst_ref=answer.at[me, pl.ds(0, 8)],
            send_sem=send_sem,
            recv_sem=recv_sem,
            device_id=device_at(DEVICES - k),
            device_id_type=MESH,
        ).start()
        return carry

    lax.fori_loop(first, last, send, 0)


SIDES = tuple((dx, dy) for dx in (-1, 0, 1) for dy in (-1, 0, 1) if (dx, dy) != (0, 0))


def halo_copies(block, strips, x_halo, y_halo, send_sem, recv_sem):
    copies = []
    for at, (dx, dy) in enumerate(SIDES):
        from_rows = {-1: pl.ds(0, HALO), 0: pl.ds(0, CX), 1: pl.ds(CX - HALO, HALO)}[dx]
        to_rows = {-1: pl.ds(ROWS - HALO, HALO), 0: pl.ds(HALO, CX), 1: pl.ds(0, HALO)}[dx]
        if dy == 0:
            source, target = block.at[:, :, from_rows, :], x_halo.at[0 if dx == 1 else 1]
        else:
            source = strips.at[0 if dy == -1 else 1, :, from_rows, :]
            target = y_halo.at[0 if dy == 1 else 1, :, to_rows, :]
        copies.append(
            pltpu.make_async_remote_copy(
                src_ref=source,
                dst_ref=target,
                send_sem=send_sem.at[at],
                recv_sem=recv_sem.at[at],
                device_id=neighbour(dx, dy),
                device_id_type=MESH,
            )
        )
    return copies


def pack_strips(block, at, strips):
    group = iota((CX, 128), 1) // HALO
    low = jnp.zeros((CX, 128), F32)
    high = jnp.zeros((CX, 128), F32)
    for k in range(NZ):
        low = jnp.where(group == k, pltpu.roll(block[at, k, :, 0:128], HALO * k, 1), low)
        high = jnp.where(group == k, pltpu.roll(block[at, k, :, CY - 128 : CY], HALO * (k + 1), 1), high)
    strips[0, at] = low
    strips[1, at] = high


def make_block(pressure_ref, conductivity_ref, porosity_ref, freeze_ref, block, strips):
    for k in range(NZ):
        freeze = freeze_ref[k]
        factor = jnp.where(freeze == 0, 1.0, jnp.where(freeze == 1, 0.2, 0.02)).astype(F32)
        block[0, k] = conductivity_ref[k] * factor
        block[1, k] = porosity_ref[k]
        block[2, k] = pressure_ref[k]
    for at in range(3):
        pack_strips(block, at, strips)


def widen(block, at, x_halo, y_halo, wide):
    lane = iota((ROWS, 128), 1)
    for k in range(NZ):
        wide[k, HALO : HALO + CX, 0:CY] = block[at, k]
        wide[k, 0:HALO, 0:CY] = x_halo[0, at, k]
        wide[k, HALO + CX : ROWS, 0:CY] = x_halo[1, at, k]
        low = pltpu.roll(y_halo[0, at], 120 - HALO * k, 1)
        high = pltpu.roll(y_halo[1, at], (128 - HALO * k) % 128, 1)
        wide[k, :, CY:LANES] = jnp.where(lane < HALO, high, jnp.where(lane >= 128 - HALO, low, 0.0))


def compact(ref, group):
    lane = iota((8, 128), 1)
    first, second, third, fourth = (ref[group * 4 + i, 0:8] for i in range(4))
    second = pltpu.roll(second, 96, 1)
    third = pltpu.roll(third, 64, 1)
    fourth = pltpu.roll(fourth, 32, 1)
    mains = (
        jnp.where(lane < 96, first, second),
        jnp.where(lane < 64, second, third),
        jnp.where(lane < 32, third, fourth),
    )
    quarter = iota((3, 128), 1) // 32
    tiles = []
    for t in range(3):
        rest = None
        for q in range(4):
            at = 4 * t + q
            piece = ref[group * 4 + at // 3, pl.ds(at % 3, 3, stride=3), :]
            if q < 3:
                piece = pltpu.roll(piece, 32 * (q + 1), 1)
            rest = piece if q == 0 else jnp.where(quarter == q, piece, rest)
        tiles.append((mains[t], rest))
    return tuple(tiles)


def places(tile):
    cell = tile[1][2:3].astype(I32)
    return cell >> 8, cell & (CY - 1)


def hot(index, size):
    rows = iota((size, index.shape[1]), 0).astype(F32).astype(BF16)
    marks = jnp.broadcast_to(index.astype(F32), (16, index.shape[1])).astype(BF16)
    marks = jnp.concatenate([marks] * (size // 16), axis=0)
    return jnp.where(rows == marks, jnp.ones((), BF16), jnp.zeros((), BF16))


def scatter_group(incoming, group, total):
    tiles = ()
    for i in range(GROUP // 4):
        tiles = tiles + compact(incoming, group * (GROUP // 4) + i)
    high_parts, low_parts, right_parts = [], [], []
    for tile in tiles:
        at_x, at_y = places(tile)
        hot_x = hot(at_x, CX)
        highs = [part.astype(BF16).astype(F32) for part in tile]
        lows = [part - high for part, high in zip(tile, highs)]
        for parts, into in ((highs, high_parts), (lows, low_parts)):
            rows = []
            for k in range(NZ):
                line = parts[0][k : k + 1] if k < 8 else parts[1][k - 8 : k - 7]
                spread = jnp.broadcast_to(line, (16, 128)).astype(BF16)
                rows += [spread * hot_x[0:16], spread * hot_x[16:32]]
            into.append(jnp.concatenate(rows, axis=0))
        right_parts.append(hot(at_y, CY))
    left = jnp.concatenate(high_parts + low_parts, axis=1)
    right = jnp.concatenate(right_parts + right_parts, axis=1)
    total[...] += lax.dot_general(left, right, (((1,), (1,)), ((), ())), preferred_element_type=F32)


def keep_source(total, mask_ref, source, strips):
    mask = mask_ref[...].astype(F32)
    for k in range(NZ):
        source[0, k] = total[k * CX : (k + 1) * CX] * mask
    pack_strips(source, 0, strips)


def up(field, dim):
    return pltpu.roll(field, field.shape[dim] - 1, dim)


def down(field, dim):
    return pltpu.roll(field, 1, dim)


def dry_inverse(field):
    dryness = jnp.maximum(-field, 0.0)
    return dryness, lax.rsqrt(1.0 + dryness * dryness)


def joined(one, two):
    both = one + two
    return one * two / jnp.where(both > 0.0, both, 1.0)


def grid_edges(wide_shape):
    gx, gy = position()
    row, lane = iota(wide_shape, 0), iota(wide_shape, 1)
    outside = ((row < HALO) & (gx == 0)) | ((row >= HALO + CX) & (gx == GX - 1))
    return outside | ((lane >= CY + 64) & (gy == 0)) | ((lane >= CY) & (lane < CY + 64) & (gy == GY - 1))


def zero_ends(p, kr, gz, u, v):
    zero = jnp.zeros((ROWS, LANES), F32)
    for ref, at in ((p, NZ), (kr, NZ), (gz, 0), (gz, NZ), (u, 0), (u, NZ + 1), (v, 0), (v, NZ + 1)):
        ref[at] = zero


def make_faces(perm, p, stored, hx, hy, hz):
    outside = grid_edges((ROWS, LANES))

    def prepare(k, carry):
        perm[k] = jnp.where(outside, 0.0, perm[k])
        return carry

    lax.fori_loop(0, NZ, prepare, 0, unroll=10)

    def faces(k, carry):
        here = perm[k]
        hx[k] = joined(here, up(here, 0))
        hy[k] = joined(here, up(here, 1))
        stored[k] = dry_inverse(p[k])[1]
        return carry

    lax.fori_loop(0, NZ, faces, 0, unroll=10)

    def vertical_faces(k, carry):
        hz[k] = joined(perm[k], perm[k + 1])
        return carry

    lax.fori_loop(0, NZ - 1, vertical_faces, 0)


def linearize(perm, porosity, p, stored, kr, hx, hy, hz, gx_, gy_, gz, scale, start):
    def relative(k, carry):
        inverse = dry_inverse(p[k])[1]
        kr[k] = inverse * inverse * inverse
        return carry

    lax.fori_loop(0, NZ, relative, 0, unroll=10)

    def layer(k, flow_above, last):
        here, rel = p[k], kr[k]
        side_x = hx[k] * (rel + up(rel, 0))
        side_y = hy[k] * (rel + up(rel, 1))
        gx_[k] = side_x
        gy_[k] = side_y
        flow_x = side_x * (here - up(here, 0))
        flow_y = side_y * (here - up(here, 1))
        above = gz[k]
        if last:
            flow = perm[k] * rel
        else:
            below = hz[k] * (rel + kr[k + 1])
            gz[k + 1] = below
            flow = below * (here - p[k + 1] + 1.0)
        dryness, inverse = dry_inverse(here)
        residual = porosity[k] * (inverse - stored[k]) + (flow_x - down(flow_x, 0)) + (flow_y - down(flow_y, 1))
        start[k] = residual + flow - flow_above
        diagonal = porosity[k] * (dryness * rel) + side_x + down(side_x, 0) + side_y + down(side_y, 1) + above
        if not last:
            diagonal = diagonal + below
        scale[k] = OMEGA / jnp.where(diagonal > 0.0, diagonal, 1.0)
        return flow

    flow = lax.fori_loop(0, NZ - 1, lambda k, f: layer(k, f, False), jnp.zeros((ROWS, LANES), F32), unroll=9)
    layer(NZ - 1, flow, True)


def smooth(p, src, gx_, gy_, gz, scale, start, u, v):
    def first(k, carry):
        opening = (src[k] - start[k]) * scale[k]
        start[k] = opening
        u[k + 1] = opening
        return carry

    lax.fori_loop(0, NZ, first, 0, unroll=10)
    for old, new in ((u, v), (v, u), (u, v)):

        def sweep(k, carry, old=old, new=new):
            here = old[k + 1]
            side_x, side_y = gx_[k], gy_[k]
            coupled = side_x * up(here, 0) + down(side_x * here, 0) + side_y * up(here, 1) + down(side_y * here, 1)
            coupled = coupled + gz[k] * old[k] + gz[k + 1] * old[k + 2]
            new[k + 1] = (1.0 - OMEGA) * here + start[k] + scale[k] * coupled
            return carry

        lax.fori_loop(0, NZ, sweep, 0, unroll=10)

    def advance(k, carry):
        p[k] = p[k] + v[k + 1]
        return carry

    lax.fori_loop(0, NZ, advance, 0, unroll=10)


def finish(p, pressure_out, saturated):
    for k in range(NZ):
        final = p[k, HALO : HALO + CX, 0:CY]
        pressure_out[k] = final
        rows = pl.ds(k, CX, stride=8) if k < 8 else pl.ds(CX * 8 + k - 8, CX, stride=2)
        sat = dry_inverse(final)[1]
        saturated[0, rows, :] = sat[:, 0:128]
        saturated[1, rows, :] = sat[:, 128:256]


def gather_group(saturated, incoming, group, reply):
    lane = iota((8, 128), 1)
    row = iota((8, 128), 0)
    every = jnp.concatenate([saturated[0], saturated[1]], axis=1)
    high = every.astype(BF16)
    left = jnp.concatenate([high, (every - high.astype(F32)).astype(BF16)], axis=1)
    for pair in range(GROUP // 8):
        at = group * (GROUP // 4) + 2 * pair
        tiles = compact(incoming, at) + compact(incoming, at + 1)
        spots = [places(tile) for tile in tiles]
        outs = []
        for i in range(3):
            two = jnp.concatenate([hot(spots[2 * i][1], CY), hot(spots[2 * i + 1][1], CY)], axis=1)
            both = jnp.concatenate([two, two], axis=0)
            lines = jnp.dot(left, both, preferred_element_type=F32)
            for half in range(2):
                part = lines[:, half * 128 : half * 128 + 128]
                at_x = jnp.broadcast_to(spots[2 * i + half][0], (8, 128))
                first = part[0:8]
                for x in range(1, CX):
                    first = jnp.where(at_x == x, part[8 * x : 8 * x + 8], first)
                second = part[256:264]
                for g in range(1, 8):
                    second = jnp.where((at_x >> 2) == g, part[256 + 8 * g : 264 + 8 * g], second)
                second = jnp.where((row >> 1) == (at_x & 3), second, 0.0)
                second = second + pltpu.roll(second, 4, 0)
                second = second + pltpu.roll(second, 2, 0)
                outs.append((first, second))
        for j in range(2):
            three = outs[3 * j : 3 * j + 3]
            mains, rests = [m for m, _ in three], [r for _, r in three]
            mains = (
                mains[0],
                pltpu.roll(jnp.where(lane >= 96, mains[0], mains[1]), 32, 1),
                pltpu.roll(jnp.where(lane >= 64, mains[1], mains[2]), 64, 1),
                pltpu.roll(mains[2], 96, 1),
            )
            for i in range(4):
                slab = mains[i]
                for third in range(3):
                    at = 3 * i + third
                    piece = rests[at // 4]
                    if at % 4 < 3:
                        piece = pltpu.roll(piece, 96 - 32 * (at % 4), 1)
                    slab = jnp.where((lane >= 96) & (row >> 1 == third), piece, slab)
                reply[group * GROUP + pair * 8 + j * 4 + i] = slab


def interval_kernel(*refs):
    given, (pressure_out, answer), held, refs = refs[:6], refs[6:8], refs[8:14], refs[14:]
    (
        incoming, reply, saturated, total, block, strips, x_halo, y_halo,
        source, source_strips, source_x, source_y,
        perm, porosity, p, src, stored, kr, hx, hy, hz, gx_, gy_, gz, scale, start, u, v,
        load_sems, sems, group_sems, halo_send, halo_recv, source_send, source_recv,
    ) = refs
    messages, mask_ref = held[0], held[5]
    loads = [pltpu.make_async_copy(one, kept, load_sems.at[i]) for i, (one, kept) in enumerate(zip(given, held))]
    for load in loads[1:] + loads[:1]:
        load.start()
    greet_all()
    for load in loads[1:]:
        load.wait()
    make_block(*held[1:5], block, strips)
    loads[0].wait()
    pl.semaphore_wait(pltpu.get_barrier_semaphore(), DEVICES - 1)
    halos = halo_copies(block, strips, x_halo, y_halo, halo_send, halo_recv)
    for group in range(GROUPS):
        send_messages(messages, incoming, group, sems.at[0], group_sems)
    for copy in halos:
        copy.start()
    gx, gy = position()
    incoming[0] = messages[gx * GY + gy]
    zero_ends(p, kr, gz, u, v)
    total[...] = jnp.zeros_like(total)
    wait_for(incoming, 1, GROUP - 1, SENT, group_sems.at[0])
    scatter_group(incoming, 0, total)

    def arrive(group, carry):
        wait_for(incoming, group * GROUP, GROUP, SENT, group_sems.at[group])
        scatter_group(incoming, group, total)
        return carry

    lax.fori_loop(1, GROUPS, arrive, 0)
    keep_source(total, mask_ref, source, source_strips)
    copies = halo_copies(source, source_strips, source_x, source_y, source_send, source_recv)
    for copy in copies:
        copy.start()
    for copy in halos:
        copy.wait_recv()
    widen(block, 0, x_halo, y_halo, perm)
    widen(block, 1, x_halo, y_halo, porosity)
    widen(block, 2, x_halo, y_halo, p)
    make_faces(perm, p, stored, hx, hy, hz)
    linearize(perm, porosity, p, stored, kr, hx, hy, hz, gx_, gy_, gz, scale, start)
    for copy in copies:
        copy.wait_recv()
    widen(source, 0, source_x, source_y, src)
    smooth(p, src, gx_, gy_, gz, scale, start, u, v)
    linearize(perm, porosity, p, stored, kr, hx, hy, hz, gx_, gy_, gz, scale, start)
    smooth(p, src, gx_, gy_, gz, scale, start, u, v)
    finish(p, pressure_out, saturated)
    gather_group(saturated, incoming, 0, reply)
    send_replies(reply, answer, 1, GROUP, sems.at[1], sems.at[2])
    gx, gy = position()
    answer[gx * GY + gy] = reply[0]

    def depart(group, carry):
        gather_group(saturated, incoming, group, reply)
        send_replies(reply, answer, group * GROUP, group * GROUP + GROUP, sems.at[1], sems.at[2])
        return carry

    lax.fori_loop(1, GROUPS, depart, 0)
    for copy in halos + copies:
        copy.wait_send()
    wait_for(messages, 1, DEVICES - 1, SENT, sems.at[0])
    wait_for(reply, 1, DEVICES - 1, 8, sems.at[1])
    wait_for(answer, 1, DEVICES - 1, 8, sems.at[2])


def shaped(*lengths):
    return jax.ShapeDtypeStruct(lengths, F32)


def call(kernel, outs, scratch, extra=None, ins=None, count=None):
    return pl.pallas_call(
        kernel,
        out_shape=outs,
        in_specs=ins or [VMEM] * count,
        out_specs=jax.tree.map(lambda _: VMEM, outs),
        scratch_shapes=scratch,
        compiler_params=params(**(extra or {})),
    )


def on_device(
    clm_block, clm_cell, precip, evap_demand, root_share, sat_before,
    pressure, conductivity, porosity, freeze_state, land_mask,
):
    flat = [a.reshape(1, COLUMNS) for a in (clm_block, clm_cell, precip, evap_demand)]
    dma = pltpu.SemaphoreType.DMA
    wide = [
        pltpu.VMEM((n, ROWS, LANES), F32)
        for n in (NZ, NZ, NZ + 1, NZ, NZ, NZ + 1, NZ, NZ, NZ, NZ, NZ, NZ + 1, NZ, NZ, NZ + 2, NZ + 2)
    ]
    memory = lambda *lengths: pltpu.VMEM(lengths, F32)
    anywhere = pl.BlockSpec(memory_space=pl.ANY)
    held = lambda given: [pltpu.VMEM(a.shape, a.dtype) for a in given]
    given = (*flat, root_share, sat_before)
    messages, ends = call(
        prep_kernel,
        (shaped(DEVICES, 16, 128), jax.ShapeDtypeStruct((8, 128), I32)),
        held(given)
        + [memory(16, COLUMNS + 256), memory(16, COLUMNS + 256), pltpu.SMEM((8, 128), I32), dma((6,)), dma],
        ins=[anywhere] * 6,
    )(*given)
    given = (messages, pressure, conductivity, porosity, freeze_state, land_mask)
    pressure_now, answer = call(
        interval_kernel,
        (shaped(NZ, CX, CY), shaped(DEVICES, 8, 128)),
        held(given)
        + [memory(DEVICES, 16, 128), memory(DEVICES, 8, 128), memory(2, NZ * CX, 128), memory(NZ * CX, CY)]
        + [memory(3, NZ, CX, CY), memory(2, 3, CX, 128), memory(2, 3, NZ, HALO, CY), memory(2, 3, ROWS, 128)]
        + [memory(1, NZ, CX, CY), memory(2, 1, CX, 128), memory(2, 1, NZ, HALO, CY), memory(2, 1, ROWS, 128)]
        + wide
        + [dma((6,)), dma((3,)), dma((GROUPS,)), dma((8,)), dma((8,)), dma((8,)), dma((8,))],
        dict(collective_id=0, has_side_effects=True),
        ins=[anywhere] * 6,
    )(*given)
    new_pressure, returned = call(
        unroute_kernel,
        (shaped(NZ, CX, CY), shaped(NZ, COLUMNS)),
        [memory(8, COLUMNS + 256), memory(8, COLUMNS + 256), memory(DEVICES * 8, 128)],
        ins=[SMEM, VMEM, VMEM],
    )(ends, answer.reshape(DEVICES * 8, 128), pressure_now)
    return new_pressure, returned


def solution(mesh):
    both = P(("gx", "gy"))
    columns = P(None, ("gx", "gy"))
    grid = P(None, "gx", "gy")
    return jax.shard_map(
        on_device,
        mesh=mesh,
        in_specs=(both, both, both, both, columns, columns, grid, grid, grid, grid, P("gx", "gy")),
        out_specs=(grid, columns),
        check_vma=False,
    )
```

```python
import functools

import jax
import jax.numpy as jnp
from jax import lax
from jax.experimental import pallas as pl
from jax.experimental.pallas import tpu as pltpu
from jax.sharding import PartitionSpec as P

MESH = pl.DeviceIdType.MESH
F32, BF16, I32 = jnp.float32, jnp.bfloat16, jnp.int32

NZ = 10
CX = 32
CY = 256
GX = 16
GY = 8
DEVICES = GX * GY
GROUP = 16
GROUPS = DEVICES // GROUP
SENT = 9
COLUMNS = CX * CY
HALO = 8
ROWS = CX + 2 * HALO
LANES = CY + 128
OMEGA = 0.8
VMEM_LIMIT = 56 * 1024 * 1024

VMEM = pl.BlockSpec(memory_space=pltpu.VMEM)
SMEM = pl.BlockSpec(memory_space=pltpu.SMEM)


def iota(shape, dim):
    return lax.broadcasted_iota(I32, shape, dim)


def params(**extra):
    return pltpu.CompilerParams(vmem_limit_bytes=VMEM_LIMIT, **extra)


def owner_ends(block_ref, row):
    owners = iota((DEVICES, 128), 0)

    def count(j, total):
        piece = block_ref[:, pl.ds(pl.multiple_of(j * 128, 128), 128)]
        return total + jnp.where(piece <= owners, 1, 0)

    total = lax.fori_loop(0, COLUMNS // 128, count, jnp.zeros((DEVICES, 128), I32), unroll=4)
    row[...] = jnp.broadcast_to(jnp.sum(total.T, axis=0, keepdims=True), (8, 128))


def column_fluxes(cell_ref, precip_ref, evap_ref, root_ref, sat_ref, payload):
    width = 512

    def chunk(j, carry):
        at = pl.ds(pl.multiple_of(j * width, width), width)
        sat = sat_ref[:, at]
        weights = root_ref[:, at] * sat * sat
        total = 0.25 + jnp.sum(weights, axis=0, keepdims=True)
        uptake = evap_ref[:, at] * weights / total
        top = sat[0:1]
        infiltration = precip_ref[:, at] * (1.0 - top * top * top)
        payload[0:NZ, at] = jnp.where(iota((NZ, width), 0) == 0, infiltration, 0.0) - uptake
        payload[NZ : NZ + 1, at] = cell_ref[:, at].astype(F32)
        return carry

    lax.fori_loop(0, COLUMNS // width, chunk, 0)
    payload[:, COLUMNS : COLUMNS + 256] = jnp.zeros((16, 256), F32)


def fold_last_rows(payload, folded):
    row, lane = iota((8, 128), 0), iota((8, 128), 1)
    third = jnp.where(row >= 6, row - 6, jnp.where(row >= 3, row - 3, row))
    moved = 96 - 32 * third

    def tile(t, carry):
        before, before_last = carry
        at = pl.ds(pl.multiple_of(t * 128, 128), 128)
        rows = [jnp.broadcast_to(payload[k : k + 1, at], (8, 128)) for k in (8, 9, 10)]
        mixed = jnp.where(row < 3, rows[0], jnp.where(row < 6, rows[1], rows[2]))
        here = jnp.where(
            third == 0, pltpu.roll(mixed, 96, 1), jnp.where(third == 1, pltpu.roll(mixed, 64, 1), pltpu.roll(mixed, 32, 1))
        )
        last = pltpu.roll(rows[2], 32, 1)
        folded[0:8, at] = jnp.where(lane < moved, before, here)
        folded[8:16, at] = jnp.where(lane < 32, before_last, last)
        return here, last

    zero = jnp.zeros((8, 128), F32)
    lax.fori_loop(0, COLUMNS // 128 + 2, tile, (zero, zero), unroll=22)


def run_of(ends, owner):
    end = ends[0, owner]
    start = jnp.where(owner == 0, 0, ends[0, jnp.maximum(owner - 1, 0)])
    base = pl.multiple_of((start // 128) * 128, 128)
    return start, end, base, start - base


def make_messages(ends, payload, folded, messages):
    lane, row = iota((8, 128), 1), iota((8, 128), 0)
    place = jnp.where(lane >= 96, lane - 96 + 32 * (row - 6), 0)
    cells = (lane >= 96) & (row >= 6)

    def one(owner, carry):
        start, end, base, shift = run_of(ends, owner)
        amount = jnp.where(shift == 0, 0, 128 - shift)
        here, there = pl.ds(base, 128), pl.ds(pl.multiple_of(base + 128, 128), 128)
        cut = shift + 96
        first = pltpu.roll(jnp.where(lane < cut, payload[0:8, here], folded[0:8, here]), amount, 1)
        second = pltpu.roll(jnp.where(lane + 128 < cut, payload[0:8, there], folded[0:8, there]), amount, 1)
        slab = jnp.where(lane < 128 - shift, first, second)
        messages[owner, 0:8] = jnp.where(cells & (place >= end - start), -1.0, slab)
        first = pltpu.roll(folded[8:16, here], amount, 1)
        second = pltpu.roll(folded[8:16, there], amount, 1)
        slab = jnp.where(lane < 128 - shift, first, second)
        messages[owner, 8:16] = jnp.where(lane - 32 >= end - start, -1.0, slab)
        return carry

    lax.fori_loop(0, DEVICES, one, 0, unroll=16)


def prep_kernel(*refs):
    given, (messages, ends_out), held = refs[:6], refs[6:8], refs[8:14]
    payload, folded, ends, load_sems, ends_sem = refs[14:]
    loads = [pltpu.make_async_copy(one, kept, load_sems.at[i]) for i, (one, kept) in enumerate(zip(given, held))]
    for load in loads:
        load.start()
    loads[0].wait()
    owner_ends(held[0], ends_out)
    copy_ends = pltpu.make_async_copy(ends_out, ends, ends_sem)
    copy_ends.start()
    for load in loads[1:]:
        load.wait()
    column_fluxes(*held[1:], payload)
    fold_last_rows(payload, folded)
    copy_ends.wait()
    make_messages(ends, payload, folded, messages)


def unroute_kernel(ends, answer_ref, pressure_ref, pressure_out, out_ref, wide, wide_last, last):
    pressure_out[...] = pressure_ref[...]
    lane = iota((DEVICES, 128), 1)
    for k in range(2):
        thirds = [
            pltpu.roll(answer_ref[pl.ds(2 * third + k, DEVICES, stride=8), :], 32 * (third + 1), 1) for third in range(3)
        ]
        last[pl.ds(k, DEVICES, stride=8), :] = jnp.where(
            lane < 32, thirds[0], jnp.where(lane < 64, thirds[1], thirds[2])
        )
    lane = iota((8, 128), 1)

    def one(owner, carry):
        tile, tile_last, before, before_last, old = carry
        _, _, base, shift = run_of(ends, owner)
        at = pl.ds(pl.multiple_of(owner * 8, 8), 8)
        slab = pltpu.roll(answer_ref[at, :], shift, 1)
        slab_last = pltpu.roll(last[at, :], shift, 1)
        here, there = pl.ds(base, 128), pl.ds(pl.multiple_of(base + 128, 128), 128)
        tile = jnp.where(lane >= shift, slab, jnp.where(base == old, tile, before))
        tile_last = jnp.where(lane >= shift, slab_last, jnp.where(base == old, tile_last, before_last))
        wide[:, here] = tile
        wide_last[:, here] = tile_last
        wide[:, there] = slab
        wide_last[:, there] = slab_last
        return tile, tile_last, slab, slab_last, base

    zero = jnp.zeros((8, 128), F32)
    lax.fori_loop(0, DEVICES, one, (zero, zero, zero, zero, jnp.int32(0)), unroll=16)
    out_ref[0:8, :] = wide[:, 0:COLUMNS]
    out_ref[8:NZ, :] = wide_last[0:2, 0:COLUMNS]


def position():
    return lax.axis_index("gx"), lax.axis_index("gy")


def device_at(offset):
    gx, gy = position()
    flat = lax.rem(gx * GY + gy + offset, DEVICES)
    return flat // GY, lax.rem(flat, GY)


def neighbour(dx, dy):
    gx, gy = position()
    return lax.rem(gx + dx + GX, GX), lax.rem(gy + dy + GY, GY)


def greet_all():
    barrier = pltpu.get_barrier_semaphore()

    def greet(k, carry):
        pl.semaphore_signal(barrier, inc=1, device_id=device_at(k), device_id_type=MESH)
        return carry

    lax.fori_loop(1, DEVICES, greet, 0)


def send_messages(messages, incoming, group, send_sem, recv_sems):
    def send(k, carry):
        to = device_at(k)
        pltpu.make_async_remote_copy(
            src_ref=messages.at[to[0] * GY + to[1], pl.ds(0, SENT)],
            dst_ref=incoming.at[k, pl.ds(0, SENT)],
            send_sem=send_sem,
            recv_sem=recv_sems.at[group],
            device_id=to,
            device_id_type=MESH,
        ).start()
        return carry

    lax.fori_loop(max(group * GROUP, 1), (group + 1) * GROUP, send, 0)


def wait_for(ref, first, count, rows, sem):
    part = ref.at[pl.ds(first, count), pl.ds(0, rows)]
    pltpu.make_async_copy(part, part, sem).wait()


def send_replies(reply, answer, first, count, send_sem, recv_sem):
    gx, gy = position()
    me = gx * GY + gy

    def send(k, carry):
        pltpu.make_async_remote_copy(
            src_ref=reply.at[k, pl.ds(0, 8)],
            dst_ref=answer.at[me, pl.ds(0, 8)],
            send_sem=send_sem,
            recv_sem=recv_sem,
            device_id=device_at(DEVICES - k),
            device_id_type=MESH,
        ).start()
        return carry

    for k in range(count):
        send(first + k, 0)


SIDES = tuple((dx, dy) for dx in (-1, 0, 1) for dy in (-1, 0, 1) if (dx, dy) != (0, 0))


def halo_copies(block, strips, x_halo, y_halo, send_sem, recv_sem):
    copies = []
    for at, (dx, dy) in enumerate(SIDES):
        from_rows = {-1: pl.ds(0, HALO), 0: pl.ds(0, CX), 1: pl.ds(CX - HALO, HALO)}[dx]
        to_rows = {-1: pl.ds(ROWS - HALO, HALO), 0: pl.ds(HALO, CX), 1: pl.ds(0, HALO)}[dx]
        if dy == 0:
            source, target = block.at[:, :, from_rows, :], x_halo.at[0 if dx == 1 else 1]
        else:
            source = strips.at[0 if dy == -1 else 1, :, from_rows, :]
            target = y_halo.at[0 if dy == 1 else 1, :, to_rows, :]
        copies.append(
            pltpu.make_async_remote_copy(
                src_ref=source,
                dst_ref=target,
                send_sem=send_sem.at[at],
                recv_sem=recv_sem.at[at],
                device_id=neighbour(dx, dy),
                device_id_type=MESH,
            )
        )
    return copies


def pack_strips(block, at, strips):
    group = iota((CX, 128), 1) // HALO
    low = jnp.zeros((CX, 128), F32)
    high = jnp.zeros((CX, 128), F32)
    for k in range(NZ):
        low = jnp.where(group == k, pltpu.roll(block[at, k, :, 0:128], HALO * k, 1), low)
        high = jnp.where(group == k, pltpu.roll(block[at, k, :, CY - 128 : CY], HALO * (k + 1), 1), high)
    strips[0, at] = low
    strips[1, at] = high


def make_block(pressure_ref, conductivity_ref, porosity_ref, freeze_ref, block, strips):
    for k in range(NZ):
        freeze = freeze_ref[k]
        factor = jnp.where(freeze == 0, 1.0, jnp.where(freeze == 1, 0.2, 0.02)).astype(F32)
        block[0, k] = conductivity_ref[k] * factor
        block[1, k] = porosity_ref[k]
        block[2, k] = pressure_ref[k]
    for at in range(3):
        pack_strips(block, at, strips)


def widen(block, at, x_halo, y_halo, wide):
    lane = iota((ROWS, 128), 1)
    for k in range(NZ):
        wide[k, HALO : HALO + CX, 0:CY] = block[at, k]
        wide[k, 0:HALO, 0:CY] = x_halo[0, at, k]
        wide[k, HALO + CX : ROWS, 0:CY] = x_halo[1, at, k]
        low = pltpu.roll(y_halo[0, at], 120 - HALO * k, 1)
        high = pltpu.roll(y_halo[1, at], (128 - HALO * k) % 128, 1)
        wide[k, :, CY:LANES] = jnp.where(lane < HALO, high, jnp.where(lane >= 128 - HALO, low, 0.0))


def compact(ref, group):
    lane = iota((8, 128), 1)
    first, second, third, fourth = (ref[group * 4 + i, 0:8] for i in range(4))
    second = pltpu.roll(second, 96, 1)
    third = pltpu.roll(third, 64, 1)
    fourth = pltpu.roll(fourth, 32, 1)
    mains = (
        jnp.where(lane < 96, first, second),
        jnp.where(lane < 64, second, third),
        jnp.where(lane < 32, third, fourth),
    )
    quarter = iota((3, 128), 1) // 32
    tiles = []
    for t in range(3):
        rest = None
        for q in range(4):
            at = 4 * t + q
            piece = ref[group * 4 + at // 3, pl.ds(at % 3, 3, stride=3), :]
            if q < 3:
                piece = pltpu.roll(piece, 32 * (q + 1), 1)
            rest = piece if q == 0 else jnp.where(quarter == q, piece, rest)
        tiles.append((mains[t], rest))
    return tuple(tiles)


def places(tile):
    cell = tile[1][2:3].astype(I32)
    return cell >> 8, cell & (CY - 1)


def hot(index, size):
    rows = iota((size, index.shape[1]), 0).astype(F32).astype(BF16)
    marks = jnp.broadcast_to(index.astype(F32), (16, index.shape[1])).astype(BF16)
    marks = jnp.concatenate([marks] * (size // 16), axis=0)
    return jnp.where(rows == marks, jnp.ones((), BF16), jnp.zeros((), BF16))


def scatter_group(incoming, group, total):
    tiles = ()
    for i in range(GROUP // 4):
        tiles = tiles + compact(incoming, group * (GROUP // 4) + i)
    high_parts, low_parts, right_parts = [], [], []
    for tile in tiles:
        at_x, at_y = places(tile)
        hot_x = hot(at_x, CX)
        highs = [part.astype(BF16).astype(F32) for part in tile]
        lows = [part - high for part, high in zip(tile, highs)]
        for parts, into in ((highs, high_parts), (lows, low_parts)):
            rows = []
            for k in range(NZ):
                line = parts[0][k : k + 1] if k < 8 else parts[1][k - 8 : k - 7]
                spread = jnp.broadcast_to(line, (16, 128)).astype(BF16)
                rows += [spread * hot_x[0:16], spread * hot_x[16:32]]
            into.append(jnp.concatenate(rows, axis=0))
        right_parts.append(hot(at_y, CY))
    left = jnp.concatenate(high_parts + low_parts, axis=1)
    right = jnp.concatenate(right_parts + right_parts, axis=1)
    total[...] += lax.dot_general(left, right, (((1,), (1,)), ((), ())), preferred_element_type=F32)


def keep_source(total, mask_ref, source, strips):
    mask = mask_ref[...].astype(F32)
    for k in range(NZ):
        source[0, k] = total[k * CX : (k + 1) * CX] * mask
    pack_strips(source, 0, strips)


def up(field, dim):
    return pltpu.roll(field, field.shape[dim] - 1, dim)


def down(field, dim):
    return pltpu.roll(field, 1, dim)


def dry_inverse(field):
    dryness = jnp.maximum(-field, 0.0)
    return dryness, lax.rsqrt(1.0 + dryness * dryness)


def joined(one, two):
    both = one + two
    return one * two / jnp.where(both > 0.0, both, 1.0)


def grid_edges(wide_shape):
    gx, gy = position()
    row, lane = iota(wide_shape, 0), iota(wide_shape, 1)
    outside = ((row < HALO) & (gx == 0)) | ((row >= HALO + CX) & (gx == GX - 1))
    return outside | ((lane >= CY + 64) & (gy == 0)) | ((lane >= CY) & (lane < CY + 64) & (gy == GY - 1))


def zero_ends(p, kr, gz, u, v):
    zero = jnp.zeros((ROWS, LANES), F32)
    for ref, at in ((p, NZ), (kr, NZ), (gz, 0), (gz, NZ), (u, 0), (u, NZ + 1), (v, 0), (v, NZ + 1)):
        ref[at] = zero


def make_faces(perm, p, stored, hx, hy, hz):
    outside = grid_edges((ROWS, LANES))

    def prepare(k, carry):
        perm[k] = jnp.where(outside, 0.0, perm[k])
        return carry

    lax.fori_loop(0, NZ, prepare, 0, unroll=10)

    def faces(k, carry):
        here = perm[k]
        hx[k] = joined(here, up(here, 0))
        hy[k] = joined(here, up(here, 1))
        stored[k] = dry_inverse(p[k])[1]
        return carry

    lax.fori_loop(0, NZ, faces, 0, unroll=10)

    def vertical_faces(k, carry):
        hz[k] = joined(perm[k], perm[k + 1])
        return carry

    lax.fori_loop(0, NZ - 1, vertical_faces, 0)


def linearize(perm, porosity, p, stored, kr, hx, hy, hz, gx_, gy_, gz, scale, start):
    def relative(k, carry):
        inverse = dry_inverse(p[k])[1]
        kr[k] = inverse * inverse * inverse
        return carry

    lax.fori_loop(0, NZ, relative, 0, unroll=10)

    def layer(k, flow_above, last):
        here, rel = p[k], kr[k]
        side_x = hx[k] * (rel + up(rel, 0))
        side_y = hy[k] * (rel + up(rel, 1))
        gx_[k] = side_x
        gy_[k] = side_y
        flow_x = side_x * (here - up(here, 0))
        flow_y = side_y * (here - up(here, 1))
        above = gz[k]
        if last:
            flow = perm[k] * rel
        else:
            below = hz[k] * (rel + kr[k + 1])
            gz[k + 1] = below
            flow = below * (here - p[k + 1] + 1.0)
        dryness, inverse = dry_inverse(here)
        residual = porosity[k] * (inverse - stored[k]) + (flow_x - down(flow_x, 0)) + (flow_y - down(flow_y, 1))
        start[k] = residual + flow - flow_above
        diagonal = porosity[k] * (dryness * rel) + side_x + down(side_x, 0) + side_y + down(side_y, 1) + above
        if not last:
            diagonal = diagonal + below
        scale[k] = OMEGA / jnp.where(diagonal > 0.0, diagonal, 1.0)
        return flow

    flow = lax.fori_loop(0, NZ - 1, lambda k, f: layer(k, f, False), jnp.zeros((ROWS, LANES), F32), unroll=9)
    layer(NZ - 1, flow, True)


def smooth(p, src, gx_, gy_, gz, scale, start, u, v):
    def first(k, carry):
        opening = (src[k] - start[k]) * scale[k]
        start[k] = opening
        u[k + 1] = opening
        return carry

    lax.fori_loop(0, NZ, first, 0, unroll=10)
    for old, new in ((u, v), (v, u), (u, v)):

        def sweep(k, carry, old=old, new=new):
            here = old[k + 1]
            side_x, side_y = gx_[k], gy_[k]
            coupled = side_x * up(here, 0) + down(side_x * here, 0) + side_y * up(here, 1) + down(side_y * here, 1)
            coupled = coupled + gz[k] * old[k] + gz[k + 1] * old[k + 2]
            new[k + 1] = (1.0 - OMEGA) * here + start[k] + scale[k] * coupled
            return carry

        lax.fori_loop(0, NZ, sweep, 0, unroll=10)

    def advance(k, carry):
        p[k] = p[k] + v[k + 1]
        return carry

    lax.fori_loop(0, NZ, advance, 0, unroll=10)


def finish(p, pressure_out, saturated):
    for k in range(NZ):
        final = p[k, HALO : HALO + CX, 0:CY]
        pressure_out[k] = final
        rows = pl.ds(k, CX, stride=8) if k < 8 else pl.ds(CX * 8 + k - 8, CX, stride=2)
        sat = dry_inverse(final)[1]
        saturated[0, rows, :] = sat[:, 0:128]
        saturated[1, rows, :] = sat[:, 128:256]


def split_lines(saturated):
    every = jnp.concatenate([saturated[0], saturated[1]], axis=1)
    high = every.astype(BF16)
    return jnp.concatenate([high, (every - high.astype(F32)).astype(BF16)], axis=1)


def gather_group(left, incoming, group, reply):
    lane = iota((8, 128), 1)
    row = iota((8, 128), 0)
    for pair in range(GROUP // 8):
        at = group * (GROUP // 4) + 2 * pair
        tiles = compact(incoming, at) + compact(incoming, at + 1)
        spots = [places(tile) for tile in tiles]
        outs = []
        for i in range(3):
            two = jnp.concatenate([hot(spots[2 * i][1], CY), hot(spots[2 * i + 1][1], CY)], axis=1)
            both = jnp.concatenate([two, two], axis=0)
            lines = jnp.dot(left, both, preferred_element_type=F32)
            for half in range(2):
                part = lines[:, half * 128 : half * 128 + 128]
                at_x = jnp.broadcast_to(spots[2 * i + half][0], (8, 128))
                first = part[0:8]
                for x in range(1, CX):
                    first = jnp.where(at_x == x, part[8 * x : 8 * x + 8], first)
                second = part[256:264]
                for g in range(1, 8):
                    second = jnp.where((at_x >> 2) == g, part[256 + 8 * g : 264 + 8 * g], second)
                second = jnp.where((row >> 1) == (at_x & 3), second, 0.0)
                second = second + pltpu.roll(second, 4, 0)
                second = second + pltpu.roll(second, 2, 0)
                outs.append((first, second))
        for j in range(2):
            three = outs[3 * j : 3 * j + 3]
            mains, rests = [m for m, _ in three], [r for _, r in three]
            mains = (
                mains[0],
                pltpu.roll(jnp.where(lane >= 96, mains[0], mains[1]), 32, 1),
                pltpu.roll(jnp.where(lane >= 64, mains[1], mains[2]), 64, 1),
                pltpu.roll(mains[2], 96, 1),
            )
            for i in range(4):
                slab = mains[i]
                for third in range(3):
                    at = 3 * i + third
                    piece = rests[at // 4]
                    if at % 4 < 3:
                        piece = pltpu.roll(piece, 96 - 32 * (at % 4), 1)
                    slab = jnp.where((lane >= 96) & (row >> 1 == third), piece, slab)
                reply[group * GROUP + pair * 8 + j * 4 + i] = slab


def interval_kernel(*refs):
    given, (pressure_out, answer), held, refs = refs[:6], refs[6:8], refs[8:14], refs[14:]
    (
        incoming, reply, saturated, total, block, strips, x_halo, y_halo,
        source, source_strips, source_x, source_y,
        perm, porosity, p, src, stored, kr, hx, hy, hz, gx_, gy_, gz, scale, start, u, v,
        load_sems, sems, group_sems, halo_send, halo_recv, source_send, source_recv,
    ) = refs
    messages, mask_ref = held[0], held[5]
    loads = [pltpu.make_async_copy(one, kept, load_sems.at[i]) for i, (one, kept) in enumerate(zip(given, held))]
    for load in loads[1:] + loads[:1]:
        load.start()
    greet_all()
    for load in loads[1:]:
        load.wait()
    make_block(*held[1:5], block, strips)
    loads[0].wait()
    pl.semaphore_wait(pltpu.get_barrier_semaphore(), DEVICES - 1)
    halos = halo_copies(block, strips, x_halo, y_halo, halo_send, halo_recv)
    for group in range(GROUPS):
        send_messages(messages, incoming, group, sems.at[0], group_sems)
    for copy in halos:
        copy.start()
    gx, gy = position()
    incoming[0] = messages[gx * GY + gy]
    zero_ends(p, kr, gz, u, v)
    total[...] = jnp.zeros_like(total)
    wait_for(incoming, 1, GROUP - 1, SENT, group_sems.at[0])
    scatter_group(incoming, 0, total)

    def arrive(group, carry):
        wait_for(incoming, group * GROUP, GROUP, SENT, group_sems.at[group])
        scatter_group(incoming, group, total)
        return carry

    lax.fori_loop(1, GROUPS, arrive, 0)
    keep_source(total, mask_ref, source, source_strips)
    copies = halo_copies(source, source_strips, source_x, source_y, source_send, source_recv)
    for copy in copies:
        copy.start()
    for copy in halos:
        copy.wait_recv()
    widen(block, 0, x_halo, y_halo, perm)
    widen(block, 1, x_halo, y_halo, porosity)
    widen(block, 2, x_halo, y_halo, p)
    make_faces(perm, p, stored, hx, hy, hz)
    linearize(perm, porosity, p, stored, kr, hx, hy, hz, gx_, gy_, gz, scale, start)
    for copy in copies:
        copy.wait_recv()
    widen(source, 0, source_x, source_y, src)
    smooth(p, src, gx_, gy_, gz, scale, start, u, v)
    linearize(perm, porosity, p, stored, kr, hx, hy, hz, gx_, gy_, gz, scale, start)
    smooth(p, src, gx_, gy_, gz, scale, start, u, v)
    finish(p, pressure_out, saturated)
    left = split_lines(saturated)
    gather_group(left, incoming, 0, reply)
    send_replies(reply, answer, 1, GROUP - 1, sems.at[1], sems.at[2])
    gather_group(left, incoming, 1, reply)
    gx, gy = position()
    answer[gx * GY + gy] = reply[0]

    def depart(group, carry):
        send_replies(reply, answer, (group - 1) * GROUP, GROUP, sems.at[1], sems.at[2])
        gather_group(left, incoming, group, reply)
        return carry

    lax.fori_loop(2, GROUPS, depart, 0)
    send_replies(reply, answer, DEVICES - GROUP, GROUP, sems.at[1], sems.at[2])
    for copy in halos + copies:
        copy.wait_send()
    wait_for(messages, 1, DEVICES - 1, SENT, sems.at[0])
    wait_for(reply, 1, DEVICES - 1, 8, sems.at[1])
    wait_for(answer, 1, DEVICES - 1, 8, sems.at[2])


def shaped(*lengths):
    return jax.ShapeDtypeStruct(lengths, F32)


def call(kernel, outs, scratch, extra=None, ins=None, count=None):
    return pl.pallas_call(
        kernel,
        out_shape=outs,
        in_specs=ins or [VMEM] * count,
        out_specs=jax.tree.map(lambda _: VMEM, outs),
        scratch_shapes=scratch,
        compiler_params=params(**(extra or {})),
    )


def on_device(
    clm_block, clm_cell, precip, evap_demand, root_share, sat_before,
    pressure, conductivity, porosity, freeze_state, land_mask,
):
    flat = [a.reshape(1, COLUMNS) for a in (clm_block, clm_cell, precip, evap_demand)]
    dma = pltpu.SemaphoreType.DMA
    wide = [
        pltpu.VMEM((n, ROWS, LANES), F32)
        for n in (NZ, NZ, NZ + 1, NZ, NZ, NZ + 1, NZ, NZ, NZ, NZ, NZ, NZ + 1, NZ, NZ, NZ + 2, NZ + 2)
    ]
    memory = lambda *lengths: pltpu.VMEM(lengths, F32)
    anywhere = pl.BlockSpec(memory_space=pl.ANY)
    held = lambda given: [pltpu.VMEM(a.shape, a.dtype) for a in given]
    given = (*flat, root_share, sat_before)
    messages, ends = call(
        prep_kernel,
        (shaped(DEVICES, 16, 128), jax.ShapeDtypeStruct((8, 128), I32)),
        held(given)
        + [memory(16, COLUMNS + 256), memory(16, COLUMNS + 256), pltpu.SMEM((8, 128), I32), dma((6,)), dma],
        ins=[anywhere] * 6,
    )(*given)
    given = (messages, pressure, conductivity, porosity, freeze_state, land_mask)
    pressure_now, answer = call(
        interval_kernel,
        (shaped(NZ, CX, CY), shaped(DEVICES, 8, 128)),
        held(given)
        + [memory(DEVICES, 16, 128), memory(DEVICES, 8, 128), memory(2, NZ * CX, 128), memory(NZ * CX, CY)]
        + [memory(3, NZ, CX, CY), memory(2, 3, CX, 128), memory(2, 3, NZ, HALO, CY), memory(2, 3, ROWS, 128)]
        + [memory(1, NZ, CX, CY), memory(2, 1, CX, 128), memory(2, 1, NZ, HALO, CY), memory(2, 1, ROWS, 128)]
        + wide
        + [dma((6,)), dma((3,)), dma((GROUPS,)), dma((8,)), dma((8,)), dma((8,)), dma((8,))],
        dict(collective_id=0, has_side_effects=True),
        ins=[anywhere] * 6,
    )(*given)
    new_pressure, returned = call(
        unroute_kernel,
        (shaped(NZ, CX, CY), shaped(NZ, COLUMNS)),
        [memory(8, COLUMNS + 256), memory(8, COLUMNS + 256), memory(DEVICES * 8, 128)],
        ins=[SMEM, VMEM, VMEM],
    )(ends, answer.reshape(DEVICES * 8, 128), pressure_now)
    return new_pressure, returned


def solution(mesh):
    both = P(("gx", "gy"))
    columns = P(None, ("gx", "gy"))
    grid = P(None, "gx", "gy")
    return jax.shard_map(
        on_device,
        mesh=mesh,
        in_specs=(both, both, both, both, columns, columns, grid, grid, grid, grid, P("gx", "gy")),
        out_specs=(grid, columns),
        check_vma=False,
    )
```

```python
import functools

import jax
import jax.numpy as jnp
from jax import lax
from jax.experimental import pallas as pl
from jax.experimental.pallas import tpu as pltpu
from jax.sharding import PartitionSpec as P

MESH = pl.DeviceIdType.MESH
F32, BF16, I32 = jnp.float32, jnp.bfloat16, jnp.int32

NZ = 10
CX = 32
CY = 256
GX = 16
GY = 8
DEVICES = GX * GY
GROUP = 16
GROUPS = DEVICES // GROUP
SENT = 9
COLUMNS = CX * CY
HALO = 8
ROWS = CX + 2 * HALO
LANES = CY + 128
OMEGA = 0.8
VMEM_LIMIT = 56 * 1024 * 1024

VMEM = pl.BlockSpec(memory_space=pltpu.VMEM)
SMEM = pl.BlockSpec(memory_space=pltpu.SMEM)


def iota(shape, dim):
    return lax.broadcasted_iota(I32, shape, dim)


def params(**extra):
    return pltpu.CompilerParams(vmem_limit_bytes=VMEM_LIMIT, **extra)


def owner_ends(block_ref, row):
    owners = iota((DEVICES, 128), 0)

    def count(j, total):
        piece = block_ref[:, pl.ds(pl.multiple_of(j * 128, 128), 128)]
        return total + jnp.where(piece <= owners, 1, 0)

    total = lax.fori_loop(0, COLUMNS // 128, count, jnp.zeros((DEVICES, 128), I32), unroll=4)
    row[...] = jnp.broadcast_to(jnp.sum(total.T, axis=0, keepdims=True), (8, 128))


def column_fluxes(cell_ref, precip_ref, evap_ref, root_ref, sat_ref, payload):
    width = 512

    def chunk(j, carry):
        at = pl.ds(pl.multiple_of(j * width, width), width)
        sat = sat_ref[:, at]
        weights = root_ref[:, at] * sat * sat
        total = 0.25 + jnp.sum(weights, axis=0, keepdims=True)
        uptake = evap_ref[:, at] * weights / total
        top = sat[0:1]
        infiltration = precip_ref[:, at] * (1.0 - top * top * top)
        payload[0:NZ, at] = jnp.where(iota((NZ, width), 0) == 0, infiltration, 0.0) - uptake
        payload[NZ : NZ + 1, at] = cell_ref[:, at].astype(F32)
        return carry

    lax.fori_loop(0, COLUMNS // width, chunk, 0)
    payload[:, COLUMNS : COLUMNS + 256] = jnp.zeros((16, 256), F32)


def fold_last_rows(payload, folded):
    row, lane = iota((8, 128), 0), iota((8, 128), 1)
    third = jnp.where(row >= 6, row - 6, jnp.where(row >= 3, row - 3, row))
    moved = 96 - 32 * third

    def tile(t, carry):
        before, before_last = carry
        at = pl.ds(pl.multiple_of(t * 128, 128), 128)
        rows = [jnp.broadcast_to(payload[k : k + 1, at], (8, 128)) for k in (8, 9, 10)]
        mixed = jnp.where(row < 3, rows[0], jnp.where(row < 6, rows[1], rows[2]))
        here = jnp.where(
            third == 0, pltpu.roll(mixed, 96, 1), jnp.where(third == 1, pltpu.roll(mixed, 64, 1), pltpu.roll(mixed, 32, 1))
        )
        last = pltpu.roll(rows[2], 32, 1)
        folded[0:8, at] = jnp.where(lane < moved, before, here)
        folded[8:16, at] = jnp.where(lane < 32, before_last, last)
        return here, last

    zero = jnp.zeros((8, 128), F32)
    lax.fori_loop(0, COLUMNS // 128 + 2, tile, (zero, zero), unroll=22)


def run_of(ends, owner):
    end = ends[0, owner]
    start = jnp.where(owner == 0, 0, ends[0, jnp.maximum(owner - 1, 0)])
    base = pl.multiple_of((start // 128) * 128, 128)
    return start, end, base, start - base


def make_messages(ends, payload, folded, messages):
    lane, row = iota((8, 128), 1), iota((8, 128), 0)
    place = jnp.where(lane >= 96, lane - 96 + 32 * (row - 6), 0)
    cells = (lane >= 96) & (row >= 6)

    def one(owner, carry):
        start, end, base, shift = run_of(ends, owner)
        amount = jnp.where(shift == 0, 0, 128 - shift)
        here, there = pl.ds(base, 128), pl.ds(pl.multiple_of(base + 128, 128), 128)
        cut = shift + 96
        first = pltpu.roll(jnp.where(lane < cut, payload[0:8, here], folded[0:8, here]), amount, 1)
        second = pltpu.roll(jnp.where(lane + 128 < cut, payload[0:8, there], folded[0:8, there]), amount, 1)
        slab = jnp.where(lane < 128 - shift, first, second)
        messages[owner, 0:8] = jnp.where(cells & (place >= end - start), -1.0, slab)
        first = pltpu.roll(folded[8:16, here], amount, 1)
        second = pltpu.roll(folded[8:16, there], amount, 1)
        slab = jnp.where(lane < 128 - shift, first, second)
        messages[owner, 8:16] = jnp.where(lane - 32 >= end - start, -1.0, slab)
        return carry

    lax.fori_loop(0, DEVICES, one, 0, unroll=16)


def prep_kernel(*refs):
    given, (messages, ends_out), held = refs[:6], refs[6:8], refs[8:14]
    payload, folded, ends, load_sems, ends_sem = refs[14:]
    loads = [pltpu.make_async_copy(one, kept, load_sems.at[i]) for i, (one, kept) in enumerate(zip(given, held))]
    for load in loads:
        load.start()
    loads[0].wait()
    owner_ends(held[0], ends_out)
    copy_ends = pltpu.make_async_copy(ends_out, ends, ends_sem)
    copy_ends.start()
    for load in loads[1:]:
        load.wait()
    column_fluxes(*held[1:], payload)
    fold_last_rows(payload, folded)
    copy_ends.wait()
    make_messages(ends, payload, folded, messages)


def unroute_kernel(ends, answer_ref, pressure_ref, pressure_out, out_ref, wide, wide_last, last):
    pressure_out[...] = pressure_ref[...]
    lane = iota((DEVICES, 128), 1)
    for k in range(2):
        thirds = [
            pltpu.roll(answer_ref[pl.ds(2 * third + k, DEVICES, stride=8), :], 32 * (third + 1), 1) for third in range(3)
        ]
        last[pl.ds(k, DEVICES, stride=8), :] = jnp.where(
            lane < 32, thirds[0], jnp.where(lane < 64, thirds[1], thirds[2])
        )
    lane = iota((8, 128), 1)

    def one(owner, carry):
        tile, tile_last, before, before_last, old = carry
        _, _, base, shift = run_of(ends, owner)
        at = pl.ds(pl.multiple_of(owner * 8, 8), 8)
        slab = pltpu.roll(answer_ref[at, :], shift, 1)
        slab_last = pltpu.roll(last[at, :], shift, 1)
        here, there = pl.ds(base, 128), pl.ds(pl.multiple_of(base + 128, 128), 128)
        tile = jnp.where(lane >= shift, slab, jnp.where(base == old, tile, before))
        tile_last = jnp.where(lane >= shift, slab_last, jnp.where(base == old, tile_last, before_last))
        wide[:, here] = tile
        wide_last[:, here] = tile_last
        wide[:, there] = slab
        wide_last[:, there] = slab_last
        return tile, tile_last, slab, slab_last, base

    zero = jnp.zeros((8, 128), F32)
    lax.fori_loop(0, DEVICES, one, (zero, zero, zero, zero, jnp.int32(0)), unroll=16)
    out_ref[0:8, :] = wide[:, 0:COLUMNS]
    out_ref[8:NZ, :] = wide_last[0:2, 0:COLUMNS]


def position():
    return lax.axis_index("gx"), lax.axis_index("gy")


def device_at(offset):
    gx, gy = position()
    return lax.rem(gx + offset // GY, GX), lax.rem(gy + lax.rem(offset, GY), GY)


def device_before(offset):
    gx, gy = position()
    return lax.rem(gx - offset // GY + GX, GX), lax.rem(gy - lax.rem(offset, GY) + GY, GY)


def neighbour(dx, dy):
    gx, gy = position()
    return lax.rem(gx + dx + GX, GX), lax.rem(gy + dy + GY, GY)


def greet_all():
    barrier = pltpu.get_barrier_semaphore()

    def greet(k, carry):
        pl.semaphore_signal(barrier, inc=1, device_id=device_at(k), device_id_type=MESH)
        return carry

    lax.fori_loop(1, DEVICES, greet, 0)


def send_messages(messages, incoming, group, send_sem, recv_sems):
    def send(k, carry):
        to = device_at(k)
        pltpu.make_async_remote_copy(
            src_ref=messages.at[to[0] * GY + to[1], pl.ds(0, SENT)],
            dst_ref=incoming.at[k, pl.ds(0, SENT)],
            send_sem=send_sem,
            recv_sem=recv_sems.at[group],
            device_id=to,
            device_id_type=MESH,
        ).start()
        return carry

    lax.fori_loop(max(group * GROUP, 1), (group + 1) * GROUP, send, 0)


def wait_for(ref, first, count, rows, sem):
    part = ref.at[pl.ds(first, count), pl.ds(0, rows)]
    pltpu.make_async_copy(part, part, sem).wait()


def send_replies(reply, answer, first, count, send_sem, recv_sem):
    gx, gy = position()
    me = gx * GY + gy

    def send(k, carry):
        pltpu.make_async_remote_copy(
            src_ref=reply.at[k, pl.ds(0, 8)],
            dst_ref=answer.at[me, pl.ds(0, 8)],
            send_sem=send_sem,
            recv_sem=recv_sem,
            device_id=device_before(k),
            device_id_type=MESH,
        ).start()
        return carry

    for k in range(count):
        send(first + k, 0)


SIDES = tuple((dx, dy) for dx in (-1, 0, 1) for dy in (-1, 0, 1) if (dx, dy) != (0, 0))


def halo_copies(block, strips, x_halo, y_halo, send_sem, recv_sem):
    copies = []
    for at, (dx, dy) in enumerate(SIDES):
        from_rows = {-1: pl.ds(0, HALO), 0: pl.ds(0, CX), 1: pl.ds(CX - HALO, HALO)}[dx]
        to_rows = {-1: pl.ds(ROWS - HALO, HALO), 0: pl.ds(HALO, CX), 1: pl.ds(0, HALO)}[dx]
        if dy == 0:
            source, target = block.at[:, :, from_rows, :], x_halo.at[0 if dx == 1 else 1]
        else:
            source = strips.at[0 if dy == -1 else 1, :, from_rows, :]
            target = y_halo.at[0 if dy == 1 else 1, :, to_rows, :]
        copies.append(
            pltpu.make_async_remote_copy(
                src_ref=source,
                dst_ref=target,
                send_sem=send_sem.at[at],
                recv_sem=recv_sem.at[at],
                device_id=neighbour(dx, dy),
                device_id_type=MESH,
            )
        )
    return copies


def pack_strips(block, at, strips):
    group = iota((CX, 128), 1) // HALO
    low = jnp.zeros((CX, 128), F32)
    high = jnp.zeros((CX, 128), F32)
    for k in range(NZ):
        low = jnp.where(group == k, pltpu.roll(block[at, k, :, 0:128], HALO * k, 1), low)
        high = jnp.where(group == k, pltpu.roll(block[at, k, :, CY - 128 : CY], HALO * (k + 1), 1), high)
    strips[0, at] = low
    strips[1, at] = high


def make_block(pressure_ref, conductivity_ref, porosity_ref, freeze_ref, block, strips):
    for k in range(NZ):
        freeze = freeze_ref[k]
        factor = jnp.where(freeze == 0, 1.0, jnp.where(freeze == 1, 0.2, 0.02)).astype(F32)
        block[0, k] = conductivity_ref[k] * factor
        block[1, k] = porosity_ref[k]
        block[2, k] = pressure_ref[k]
    for at in range(3):
        pack_strips(block, at, strips)


def widen(block, at, x_halo, y_halo, wide):
    lane = iota((ROWS, 128), 1)
    for k in range(NZ):
        wide[k, HALO : HALO + CX, 0:CY] = block[at, k]
        wide[k, 0:HALO, 0:CY] = x_halo[0, at, k]
        wide[k, HALO + CX : ROWS, 0:CY] = x_halo[1, at, k]
        low = pltpu.roll(y_halo[0, at], 120 - HALO * k, 1)
        high = pltpu.roll(y_halo[1, at], (128 - HALO * k) % 128, 1)
        wide[k, :, CY:LANES] = jnp.where(lane < HALO, high, jnp.where(lane >= 128 - HALO, low, 0.0))


def compact(ref, group):
    lane = iota((8, 128), 1)
    first, second, third, fourth = (ref[group * 4 + i, 0:8] for i in range(4))
    second = pltpu.roll(second, 96, 1)
    third = pltpu.roll(third, 64, 1)
    fourth = pltpu.roll(fourth, 32, 1)
    mains = (
        jnp.where(lane < 96, first, second),
        jnp.where(lane < 64, second, third),
        jnp.where(lane < 32, third, fourth),
    )
    quarter = iota((3, 128), 1) // 32
    tiles = []
    for t in range(3):
        rest = None
        for q in range(4):
            at = 4 * t + q
            piece = ref[group * 4 + at // 3, pl.ds(at % 3, 3, stride=3), :]
            if q < 3:
                piece = pltpu.roll(piece, 32 * (q + 1), 1)
            rest = piece if q == 0 else jnp.where(quarter == q, piece, rest)
        tiles.append((mains[t], rest))
    return tuple(tiles)


def places(tile):
    cell = tile[1][2:3].astype(I32)
    return cell >> 8, cell & (CY - 1)


def hot(index, size):
    rows = iota((size, index.shape[1]), 0).astype(F32).astype(BF16)
    marks = jnp.broadcast_to(index.astype(F32), (16, index.shape[1])).astype(BF16)
    marks = jnp.concatenate([marks] * (size // 16), axis=0)
    return jnp.where(rows == marks, jnp.ones((), BF16), jnp.zeros((), BF16))


def scatter_group(incoming, group, total):
    tiles = ()
    for i in range(GROUP // 4):
        tiles = tiles + compact(incoming, group * (GROUP // 4) + i)
    high_parts, low_parts, right_parts = [], [], []
    for tile in tiles:
        at_x, at_y = places(tile)
        hot_x = hot(at_x, CX)
        highs = [part.astype(BF16).astype(F32) for part in tile]
        lows = [part - high for part, high in zip(tile, highs)]
        for parts, into in ((highs, high_parts), (lows, low_parts)):
            rows = []
            for k in range(NZ):
                line = parts[0][k : k + 1] if k < 8 else parts[1][k - 8 : k - 7]
                spread = jnp.broadcast_to(line, (16, 128)).astype(BF16)
                rows += [spread * hot_x[0:16], spread * hot_x[16:32]]
            into.append(jnp.concatenate(rows, axis=0))
        right_parts.append(hot(at_y, CY))
    left = jnp.concatenate(high_parts + low_parts, axis=1)
    right = jnp.concatenate(right_parts + right_parts, axis=1)
    total[...] += lax.dot_general(left, right, (((1,), (1,)), ((), ())), preferred_element_type=F32)


def keep_source(total, mask_ref, source, strips):
    mask = mask_ref[...].astype(F32)
    for k in range(NZ):
        source[0, k] = total[k * CX : (k + 1) * CX] * mask
    pack_strips(source, 0, strips)


def up(field, dim):
    return pltpu.roll(field, field.shape[dim] - 1, dim)


def down(field, dim):
    return pltpu.roll(field, 1, dim)


def dry_inverse(field):
    dryness = jnp.maximum(-field, 0.0)
    return dryness, lax.rsqrt(1.0 + dryness * dryness)


def joined(one, two):
    both = one + two
    return one * two / jnp.where(both > 0.0, both, 1.0)


def grid_edges(wide_shape):
    gx, gy = position()
    row, lane = iota(wide_shape, 0), iota(wide_shape, 1)
    outside = ((row < HALO) & (gx == 0)) | ((row >= HALO + CX) & (gx == GX - 1))
    return outside | ((lane >= CY + 64) & (gy == 0)) | ((lane >= CY) & (lane < CY + 64) & (gy == GY - 1))


def zero_ends(p, kr, gz, u, v):
    zero = jnp.zeros((ROWS, LANES), F32)
    for ref, at in ((p, NZ), (kr, NZ), (gz, 0), (gz, NZ), (u, 0), (u, NZ + 1), (v, 0), (v, NZ + 1)):
        ref[at] = zero


def make_faces(perm, p, stored, hx, hy, hz):
    outside = grid_edges((ROWS, LANES))

    def prepare(k, carry):
        perm[k] = jnp.where(outside, 0.0, perm[k])
        return carry

    lax.fori_loop(0, NZ, prepare, 0, unroll=10)

    def faces(k, carry):
        here = perm[k]
        hx[k] = joined(here, up(here, 0))
        hy[k] = joined(here, up(here, 1))
        stored[k] = dry_inverse(p[k])[1]
        return carry

    lax.fori_loop(0, NZ, faces, 0, unroll=10)

    def vertical_faces(k, carry):
        hz[k] = joined(perm[k], perm[k + 1])
        return carry

    lax.fori_loop(0, NZ - 1, vertical_faces, 0)


def linearize(perm, porosity, p, stored, kr, hx, hy, hz, gx_, gy_, gz, scale, start):
    def relative(k, carry):
        inverse = dry_inverse(p[k])[1]
        kr[k] = inverse * inverse * inverse
        return carry

    lax.fori_loop(0, NZ, relative, 0, unroll=10)

    def layer(k, flow_above, last):
        here, rel = p[k], kr[k]
        side_x = hx[k] * (rel + up(rel, 0))
        side_y = hy[k] * (rel + up(rel, 1))
        gx_[k] = side_x
        gy_[k] = side_y
        flow_x = side_x * (here - up(here, 0))
        flow_y = side_y * (here - up(here, 1))
        above = gz[k]
        if last:
            flow = perm[k] * rel
        else:
            below = hz[k] * (rel + kr[k + 1])
            gz[k + 1] = below
            flow = below * (here - p[k + 1] + 1.0)
        dryness, inverse = dry_inverse(here)
        residual = porosity[k] * (inverse - stored[k]) + (flow_x - down(flow_x, 0)) + (flow_y - down(flow_y, 1))
        start[k] = residual + flow - flow_above
        diagonal = porosity[k] * (dryness * rel) + side_x + down(side_x, 0) + side_y + down(side_y, 1) + above
        if not last:
            diagonal = diagonal + below
        scale[k] = OMEGA / jnp.where(diagonal > 0.0, diagonal, 1.0)
        return flow

    flow = lax.fori_loop(0, NZ - 1, lambda k, f: layer(k, f, False), jnp.zeros((ROWS, LANES), F32), unroll=9)
    layer(NZ - 1, flow, True)


def smooth(p, src, gx_, gy_, gz, scale, start, u, v):
    def first(k, carry):
        opening = (src[k] - start[k]) * scale[k]
        start[k] = opening
        u[k + 1] = opening
        return carry

    lax.fori_loop(0, NZ, first, 0, unroll=10)
    for old, new in ((u, v), (v, u), (u, v)):

        def sweep(k, carry, old=old, new=new):
            here = old[k + 1]
            side_x, side_y = gx_[k], gy_[k]
            coupled = side_x * up(here, 0) + down(side_x * here, 0) + side_y * up(here, 1) + down(side_y * here, 1)
            coupled = coupled + gz[k] * old[k] + gz[k + 1] * old[k + 2]
            new[k + 1] = (1.0 - OMEGA) * here + start[k] + scale[k] * coupled
            return carry

        lax.fori_loop(0, NZ, sweep, 0, unroll=10)

    def advance(k, carry):
        p[k] = p[k] + v[k + 1]
        return carry

    lax.fori_loop(0, NZ, advance, 0, unroll=10)


def finish(p, pressure_out, saturated):
    for k in range(NZ):
        final = p[k, HALO : HALO + CX, 0:CY]
        pressure_out[k] = final
        rows = pl.ds(k, CX, stride=8) if k < 8 else pl.ds(CX * 8 + k - 8, CX, stride=2)
        sat = dry_inverse(final)[1]
        saturated[0, rows, :] = sat[:, 0:128]
        saturated[1, rows, :] = sat[:, 128:256]


def split_lines(saturated):
    every = jnp.concatenate([saturated[0], saturated[1]], axis=1)
    high = every.astype(BF16)
    return jnp.concatenate([high, (every - high.astype(F32)).astype(BF16)], axis=1)


def gather_group(left, incoming, group, reply):
    lane = iota((8, 128), 1)
    row = iota((8, 128), 0)
    for pair in range(GROUP // 8):
        at = group * (GROUP // 4) + 2 * pair
        tiles = compact(incoming, at) + compact(incoming, at + 1)
        spots = [places(tile) for tile in tiles]
        outs = []
        for i in range(3):
            two = jnp.concatenate([hot(spots[2 * i][1], CY), hot(spots[2 * i + 1][1], CY)], axis=1)
            both = jnp.concatenate([two, two], axis=0)
            lines = jnp.dot(left, both, preferred_element_type=F32)
            for half in range(2):
                part = lines[:, half * 128 : half * 128 + 128]
                at_x = jnp.broadcast_to(spots[2 * i + half][0], (8, 128))
                first = part[0:8]
                for x in range(1, CX):
                    first = jnp.where(at_x == x, part[8 * x : 8 * x + 8], first)
                second = part[256:264]
                for g in range(1, 8):
                    second = jnp.where((at_x >> 2) == g, part[256 + 8 * g : 264 + 8 * g], second)
                second = jnp.where((row >> 1) == (at_x & 3), second, 0.0)
                second = second + pltpu.roll(second, 4, 0)
                second = second + pltpu.roll(second, 2, 0)
                outs.append((first, second))
        for j in range(2):
            three = outs[3 * j : 3 * j + 3]
            mains, rests = [m for m, _ in three], [r for _, r in three]
            mains = (
                mains[0],
                pltpu.roll(jnp.where(lane >= 96, mains[0], mains[1]), 32, 1),
                pltpu.roll(jnp.where(lane >= 64, mains[1], mains[2]), 64, 1),
                pltpu.roll(mains[2], 96, 1),
            )
            for i in range(4):
                slab = mains[i]
                for third in range(3):
                    at = 3 * i + third
                    piece = rests[at // 4]
                    if at % 4 < 3:
                        piece = pltpu.roll(piece, 96 - 32 * (at % 4), 1)
                    slab = jnp.where((lane >= 96) & (row >> 1 == third), piece, slab)
                reply[group * GROUP + pair * 8 + j * 4 + i] = slab


def interval_kernel(*refs):
    given, (pressure_out, answer), held, refs = refs[:6], refs[6:8], refs[8:14], refs[14:]
    (
        incoming, reply, saturated, total, block, strips, x_halo, y_halo,
        source, source_strips, source_x, source_y,
        perm, porosity, p, src, stored, kr, hx, hy, hz, gx_, gy_, gz, scale, start, u, v,
        load_sems, sems, group_sems, halo_send, halo_recv, source_send, source_recv,
    ) = refs
    messages, mask_ref = held[0], held[5]
    loads = [pltpu.make_async_copy(one, kept, load_sems.at[i]) for i, (one, kept) in enumerate(zip(given, held))]
    for load in loads[1:] + loads[:1]:
        load.start()
    greet_all()
    for load in loads[1:]:
        load.wait()
    make_block(*held[1:5], block, strips)
    loads[0].wait()
    pl.semaphore_wait(pltpu.get_barrier_semaphore(), DEVICES - 1)
    halos = halo_copies(block, strips, x_halo, y_halo, halo_send, halo_recv)
    for group in range(GROUPS):
        send_messages(messages, incoming, group, sems.at[0], group_sems)
    for copy in halos:
        copy.start()
    gx, gy = position()
    incoming[0] = messages[gx * GY + gy]
    zero_ends(p, kr, gz, u, v)
    total[...] = jnp.zeros_like(total)
    wait_for(incoming, 1, GROUP - 1, SENT, group_sems.at[0])
    scatter_group(incoming, 0, total)

    def arrive(group, carry):
        wait_for(incoming, group * GROUP, GROUP, SENT, group_sems.at[group])
        scatter_group(incoming, group, total)
        return carry

    lax.fori_loop(1, GROUPS, arrive, 0)
    keep_source(total, mask_ref, source, source_strips)
    copies = halo_copies(source, source_strips, source_x, source_y, source_send, source_recv)
    for copy in copies:
        copy.start()
    for copy in halos:
        copy.wait_recv()
    widen(block, 0, x_halo, y_halo, perm)
    widen(block, 1, x_halo, y_halo, porosity)
    widen(block, 2, x_halo, y_halo, p)
    make_faces(perm, p, stored, hx, hy, hz)
    linearize(perm, porosity, p, stored, kr, hx, hy, hz, gx_, gy_, gz, scale, start)
    for copy in copies:
        copy.wait_recv()
    widen(source, 0, source_x, source_y, src)
    smooth(p, src, gx_, gy_, gz, scale, start, u, v)
    linearize(perm, porosity, p, stored, kr, hx, hy, hz, gx_, gy_, gz, scale, start)
    smooth(p, src, gx_, gy_, gz, scale, start, u, v)
    finish(p, pressure_out, saturated)
    left = split_lines(saturated)
    gather_group(left, incoming, 0, reply)
    send_replies(reply, answer, 1, GROUP - 1, sems.at[1], sems.at[2])
    gather_group(left, incoming, 1, reply)
    gx, gy = position()
    answer[gx * GY + gy] = reply[0]

    def depart(group, carry):
        send_replies(reply, answer, (group - 1) * GROUP, GROUP, sems.at[1], sems.at[2])
        gather_group(left, incoming, group, reply)
        return carry

    lax.fori_loop(2, GROUPS, depart, 0)
    send_replies(reply, answer, DEVICES - GROUP, GROUP, sems.at[1], sems.at[2])
    for copy in halos + copies:
        copy.wait_send()
    wait_for(messages, 1, DEVICES - 1, SENT, sems.at[0])
    wait_for(reply, 1, DEVICES - 1, 8, sems.at[1])
    wait_for(answer, 1, DEVICES - 1, 8, sems.at[2])


def shaped(*lengths):
    return jax.ShapeDtypeStruct(lengths, F32)


def call(kernel, outs, scratch, extra=None, ins=None, count=None):
    return pl.pallas_call(
        kernel,
        out_shape=outs,
        in_specs=ins or [VMEM] * count,
        out_specs=jax.tree.map(lambda _: VMEM, outs),
        scratch_shapes=scratch,
        compiler_params=params(**(extra or {})),
    )


def on_device(
    clm_block, clm_cell, precip, evap_demand, root_share, sat_before,
    pressure, conductivity, porosity, freeze_state, land_mask,
):
    flat = [a.reshape(1, COLUMNS) for a in (clm_block, clm_cell, precip, evap_demand)]
    dma = pltpu.SemaphoreType.DMA
    wide = [
        pltpu.VMEM((n, ROWS, LANES), F32)
        for n in (NZ, NZ, NZ + 1, NZ, NZ, NZ + 1, NZ, NZ, NZ, NZ, NZ, NZ + 1, NZ, NZ, NZ + 2, NZ + 2)
    ]
    memory = lambda *lengths: pltpu.VMEM(lengths, F32)
    anywhere = pl.BlockSpec(memory_space=pl.ANY)
    held = lambda given: [pltpu.VMEM(a.shape, a.dtype) for a in given]
    given = (*flat, root_share, sat_before)
    messages, ends = call(
        prep_kernel,
        (shaped(DEVICES, 16, 128), jax.ShapeDtypeStruct((8, 128), I32)),
        held(given)
        + [memory(16, COLUMNS + 256), memory(16, COLUMNS + 256), pltpu.SMEM((8, 128), I32), dma((6,)), dma],
        ins=[anywhere] * 6,
    )(*given)
    given = (messages, pressure, conductivity, porosity, freeze_state, land_mask)
    pressure_now, answer = call(
        interval_kernel,
        (shaped(NZ, CX, CY), shaped(DEVICES, 8, 128)),
        held(given)
        + [memory(DEVICES, 16, 128), memory(DEVICES, 8, 128), memory(2, NZ * CX, 128), memory(NZ * CX, CY)]
        + [memory(3, NZ, CX, CY), memory(2, 3, CX, 128), memory(2, 3, NZ, HALO, CY), memory(2, 3, ROWS, 128)]
        + [memory(1, NZ, CX, CY), memory(2, 1, CX, 128), memory(2, 1, NZ, HALO, CY), memory(2, 1, ROWS, 128)]
        + wide
        + [dma((6,)), dma((3,)), dma((GROUPS,)), dma((8,)), dma((8,)), dma((8,)), dma((8,))],
        dict(collective_id=0, has_side_effects=True),
        ins=[anywhere] * 6,
    )(*given)
    new_pressure, returned = call(
        unroute_kernel,
        (shaped(NZ, CX, CY), shaped(NZ, COLUMNS)),
        [memory(8, COLUMNS + 256), memory(8, COLUMNS + 256), memory(DEVICES * 8, 128)],
        ins=[SMEM, VMEM, VMEM],
    )(ends, answer.reshape(DEVICES * 8, 128), pressure_now)
    return new_pressure, returned


def solution(mesh):
    both = P(("gx", "gy"))
    columns = P(None, ("gx", "gy"))
    grid = P(None, "gx", "gy")
    return jax.shard_map(
        on_device,
        mesh=mesh,
        in_specs=(both, both, both, both, columns, columns, grid, grid, grid, grid, P("gx", "gy")),
        out_specs=(grid, columns),
        check_vma=False,
    )
```
